512 devices in a mesh: node: 32 (over z, x), dev: 16 (over y, core).
Axes of the slice: x: 4, y: 8, z: 8, core: 2. Of those that a mesh axis runs over, the one named last changes fastest.
Arguments:
- tokens: bfloat16 [65536, 8192], P(('node', 'dev')), may hold values from -24 to 24
- queries: bfloat16 [65536, 1024], P(('node', 'dev')), may hold values from -20 to 20
- grad_out: bfloat16 [65536, 1024], P(('node', 'dev')), may hold values from -6 to 6
- seg_ids: int32 [512, 128], P(('node', 'dev')), may hold values from 0 to 3, never falling along the last dimension, each value on 1 to 64 neighbouring positions
- w_values: bfloat16 [8192, 256], P(('node', 'dev')), may hold values from -0.0625 to 0.0625
- w_scales: bfloat16 [4], replicated, may hold values from 0.5 to 2
Outputs:
- attn_out: bfloat16 [65536, 1024], P(('node', 'dev'))
- grad_tokens: bfloat16 [65536, 8192], P(('node', 'dev'))
- grad_weight: float32 [8192, 256], P(('node', 'dev'))
The draws below stay inside these ranges and needn't reach their ends.
Inputs may be any that keep to these rules, and one draw needn't show every extreme that they name: `seg_ids`: each device's document numbers never fall along its tokens, each document holds 1 to 64 tokens and one holds exactly that many.
All inputs are finite; a program needn't handle non-finite values.
Results may differ from the reference program's by a relative error of at most 0.024.
Values may be sent and summed in bfloat16 or wider, within the bound.
A program may use at most 64 MiB of HBM per device.

```python
import math
import jax
import jax.numpy as jnp
import numpy as np
from jax import lax

D = 8192
HD = 128
GH = 8
GROUPS = 1
RB = 2048
SEGS = 4
TOK_DEV = 128
DEVS = 512
TOKENS = 65536
N_NODE = 32
N_DEV = 16


def draw_queries(key, part):
    key = jax.random.fold_in(key, 11)
    key_base = jax.random.fold_in(key, 0)
    array_shape = (TOKENS, GROUPS * GH * HD)
    values_drawn = jnp.clip(jax.random.normal(key_base, array_shape, jnp.float32), -6.0, 6.0)
    return values_drawn.astype(jnp.bfloat16)


def strengthened(drawn, key, source, target, blocks, factor):
    owner, partner = [(jnp.arange(drawn.shape[axis_at]) // (drawn.shape[axis_at] // blocks)).reshape([-1 if axis == axis_at else 1 for axis in range(drawn.ndim)]) for axis_at in (source, target)]
    chosen = jax.random.permutation(key, blocks)[partner]
    strong = (owner == chosen) | (owner == (partner + blocks // 2) % blocks)
    return jnp.where(strong, factor * drawn, drawn)


def block_scale(stream_key, extent, cuts, smallest, top_value):
    def one(dim, blocks):
        heights = jax.random.uniform(jax.random.fold_in(jax.random.fold_in(stream_key, 6), dim), (blocks,), jnp.float32, smallest / len(cuts), top_value / len(cuts))
        return jnp.repeat(jnp.exp(heights), extent[dim] // blocks).reshape((-1,) + (1,) * (len(extent) - dim - 1))

    level = one(*cuts[0])
    for cut in cuts[1:]:
        level = level * one(*cut)
    return level


def length_profile(amount, total, limit, lean):
    weights = [(1 << 20) // math.isqrt(standing ** lean) + 1 for standing in range(2, amount + 1)]
    spare, holding = total - limit - (amount - 1), [1] * (amount - 1)
    while spare > 0:
        candidates = [i for i in range(amount - 1) if holding[i] < limit]
        pool, budget = sum([weights[i] for i in candidates]), spare
        for i in candidates:
            addition = min(limit - holding[i], max(1, budget * weights[i] // pool), spare)
            holding[i] = holding[i] + addition
            spare = spare - addition
    return np.array([limit] + holding)


def uneven_parts(stream_key, count, total, bound, skew):
    if count == 2:
        one = jax.random.randint(stream_key, (), max(1, total - bound), min(bound, total - 1) + 1)
        return jnp.stack([one, total - one])
    sizes = jnp.asarray(length_profile(count, total, bound, skew), jnp.int32)
    pairs = (count - 1) // 2
    donor, taker = sizes[1:1 + 2 * pairs:2], sizes[2:2 + 2 * pairs:2]
    room = jnp.minimum(donor - 1, bound - taker)
    passed = jax.random.randint(jax.random.fold_in(stream_key, 1), (pairs,), 0, 1 << 20) % (room + 1)
    sizes = sizes.at[1:1 + 2 * pairs:2].set(donor - passed).at[2:2 + 2 * pairs:2].set(taker + passed)
    return sizes[jax.random.permutation(jax.random.fold_in(stream_key, 2), count)]


def centred(rng, extent, width, reach, shards=(), dtype=jnp.bfloat16):
    drawn = jax.random.normal(rng, extent, jnp.float32) * width
    if len(shards) > 0:
        drawn = block_scale(rng, extent, shards, -0.22, 0.18) * drawn
    return jnp.clip(drawn, min=-reach, max=reach).astype(dtype)


def gaussian_with(own_key, extent, width, most, pieces, heavy, dtype=jnp.bfloat16):
    values = width * jax.random.normal(own_key, extent, jnp.float32)
    if pieces:
        values = values * block_scale(own_key, extent, pieces, -0.22, 0.18)
    return jnp.clip(strengthened(values, jax.random.fold_in(own_key, 3), *heavy), -most, most).astype(dtype)


def setup_inputs(seed: int = 0) -> dict:
    streams_of = jax.random.split(jax.random.key(seed), 7)
    tokens = gaussian_with(streams_of[0], (TOKENS, D), 1.0, 24.0, ((0, 512),), (0, 1, 512, 6.0))
    queries = draw_queries(jax.random.fold_in(streams_of[6], 71), 0)
    grad_out = centred(streams_of[2], (TOKENS, GROUPS * GH * HD), 1.0, 6.0, ((0, 512),))
    seg_ids = jax.vmap(lambda own: jnp.searchsorted(jnp.cumsum(uneven_parts(own, SEGS, TOK_DEV, TOK_DEV // 2, 2)), jnp.arange(TOK_DEV), side="right"))(jax.random.split(streams_of[3], DEVS)).reshape((DEVS, TOK_DEV)).astype(jnp.int32)
    w_values = centred(streams_of[4], (D, 2 * GROUPS * HD), D ** -0.5, 0.0625, ((0, 512),))
    w_scales = jnp.clip(jnp.exp(jax.random.uniform(streams_of[5], (D // RB,), jnp.float32, math.log(0.5), math.log(2.0))), 0.5, 2.0).astype(jnp.bfloat16)
    return {"tokens": tokens, "queries": queries, "grad_out": grad_out, "seg_ids": seg_ids, "w_values": w_values, "w_scales": w_scales}


def dequantize(stored, scales):
    rows_all, cols_all = stored.shape
    grouped = stored.reshape(rows_all // RB, RB, cols_all).astype(jnp.float32)
    scaled = grouped * scales.astype(jnp.float32)[:, None, None]
    return scaled.reshape(rows_all, cols_all).astype(jnp.bfloat16)


def attend(queries, keys, values, segments, cotangent):
    count = queries.shape[0]
    query_heads = queries.reshape(count, GROUPS, GH, HD).astype(jnp.float32)
    key_heads = keys.reshape(count, GROUPS, HD).astype(jnp.float32)
    value_heads = values.reshape(count, GROUPS, HD).astype(jnp.float32)
    score_scale = HD ** -0.5
    scores = jnp.einsum("tgha,sga->ghts", query_heads, key_heads) * score_scale
    positions = jnp.arange(count)
    allowed = (positions[None, :] <= positions[:, None]) & (segments[:, None] == segments[None, :])
    scores = jnp.where(allowed, scores, -1e30)
    row_top = jnp.max(scores, axis=-1, keepdims=True)
    expanded = jnp.where(allowed, jnp.exp(scores - row_top), 0.0)
    probability = expanded / jnp.sum(expanded, axis=-1, keepdims=True)
    probs_low = probability.astype(jnp.bfloat16).astype(jnp.float32)
    attended = jnp.einsum("ghts,sga->tgha", probs_low, value_heads)
    attended = attended.reshape(count, -1).astype(jnp.bfloat16)
    cot_heads = cotangent.reshape(count, GROUPS, GH, HD).astype(jnp.float32)
    grad_values = jnp.einsum("ghts,tgha->sga", probs_low, cot_heads)
    grad_probs = jnp.einsum("tgha,sga->ghts", cot_heads, value_heads)
    inner = jnp.sum(probability * grad_probs, axis=-1, keepdims=True)
    grad_scores = (probability * (grad_probs - inner) * score_scale).astype(jnp.bfloat16).astype(jnp.float32)
    grad_keys = jnp.einsum("ghts,tgha->sga", grad_scores, query_heads)
    grad_kv = jnp.concatenate([grad_keys.reshape(count, -1), grad_values.reshape(count, -1)], axis=1)
    return attended, grad_kv.astype(jnp.bfloat16)


def device_work(weight, block_tokens, block_queries, block_cot, block_segs):
    key_width = GROUPS * HD
    keys_values = jnp.dot(block_tokens, weight, preferred_element_type=jnp.float32).astype(jnp.bfloat16)
    attended, grad_kv = attend(block_queries, keys_values[:, :key_width], keys_values[:, key_width:], block_segs, block_cot)
    grad_block = lax.dot_general(grad_kv, weight, (((1,), (1,)), ((), ())), preferred_element_type=jnp.float32).astype(jnp.bfloat16)
    partial_value = lax.dot_general(block_tokens, grad_kv, (((0,), (0,)), ((), ())), preferred_element_type=jnp.float32).astype(jnp.bfloat16)
    return attended, grad_block, partial_value


def reference(tokens, queries, grad_out, seg_ids, w_values, w_scales):
    weight = dequantize(w_values, w_scales)
    all_tokens = tokens.reshape(N_NODE, N_DEV, TOK_DEV, D)
    all_queries = queries.reshape(N_NODE, N_DEV, TOK_DEV, GROUPS * GH * HD)
    all_cot = grad_out.reshape(N_NODE, N_DEV, TOK_DEV, GROUPS * GH * HD)
    all_segs = seg_ids.reshape(N_NODE, N_DEV, TOK_DEV)

    def node_step(running, packed):
        attended, grad_block, partial_value = lax.map(lambda item: device_work(weight, *item), packed)
        node_group = jnp.sum(partial_value.astype(jnp.float32), axis=0).astype(jnp.bfloat16)
        return running + node_group.astype(jnp.float32), (attended, grad_block)

    start = jnp.zeros((D, 2 * GROUPS * HD), jnp.float32)
    grad_weight, (attended, grad_blocks) = lax.scan(node_step, start, (all_tokens, all_queries, all_cot, all_segs))
    attn_out = attended.reshape(TOKENS, GROUPS * GH * HD)
    grad_tokens = grad_blocks.reshape(TOKENS, D)
    return attn_out, grad_tokens, grad_weight
```

```python
import functools
import jax
import jax.numpy as jnp
from jax import lax
from jax.experimental import pallas as pl
from jax.experimental.pallas import tpu as pltpu
from jax.sharding import PartitionSpec as P

HD = 128
GH = 8
NX, NY, NZ = 4, 8, 8
TOK = 128
D = 8192
HALF = D // 2
BLK = HALF // NZ
SCALE = HD ** (-0.5)
MESH = pl.DeviceIdType.MESH
F32, BF16 = jnp.float32, jnp.bfloat16
NT = (((1,), (1,)), ((), ()))
TN = (((0,), (0,)), ((), ()))
NN = (((1,), (0,)), ((), ()))


def dot(a, b, dims=NN):
    return lax.dot_general(a, b, dims, preferred_element_type=F32)


def wait_bytes(ref, sem):
    pltpu.make_async_copy(ref, ref, sem).wait()


def kernel(
    tok, q_hbm, go_hbm, seg, w, scales,
    attn, gtok, gw,
    X, XT, W, GT, qv, gov, plow_s, sh, kvs, kvr, G, SB, RB, YS, YR, XS, XR,
    l_sem, tok_sem, ag_x_send, ag_x_recv, ag_d_send, ag_d_recv, ag_send, ag_recv,
    kv_sem, g_sem, gt_sem, rs_send, rs_recv, rs_d_send, rs_d_recv, rs_x_send, rs_x_recv,
):
    node, dev = lax.axis_index("node"), lax.axis_index("dev")
    z, x = node // NX, node % NX
    y, c = dev // 2, dev % 2
    other = 1 - c

    def at(x, y, z, c):
        return {"node": z * NX + x, "dev": y * 2 + c}

    def remote(src, dst, ss, rs, target):
        return pltpu.make_async_remote_copy(
            src_ref=src, dst_ref=dst, send_sem=ss, recv_sem=rs, device_id=target, device_id_type=MESH
        )

    def cols(zz, core):
        return pl.ds(pl.multiple_of(zz * 2 * BLK + core * BLK, BLK), BLK)

    mine = pl.ds(pl.multiple_of(c * TOK, TOK), TOK)
    theirs = pl.ds(pl.multiple_of(other * TOK, TOK), TOK)

    bar = pltpu.get_barrier_semaphore()
    for k in range(1, 2 * NX):
        xx = (x + k // 2) % NX
        cc = (c + k % 2) % 2
        pl.semaphore_signal(bar, inc=1, device_id=at(xx, y, z, cc), device_id_type=MESH)
    for k in range(1, NY):
        pl.semaphore_signal(bar, inc=1, device_id=at(x, (y + k) % NY, z, c), device_id_type=MESH)
    for k in range(1, NZ):
        pl.semaphore_signal(bar, inc=1, device_id=at(x, y, (z + k) % NZ, c), device_id_type=MESH)

    for zz in range(NZ):
        pltpu.make_async_copy(tok.at[:, cols(zz, c)], X.at[zz, mine], l_sem.at[0]).start()
    q_copy = pltpu.make_async_copy(q_hbm, qv, l_sem.at[1])
    go_copy = pltpu.make_async_copy(go_hbm, gov, l_sem.at[2])
    q_copy.start()
    go_copy.start()

    pick = lax.broadcasted_iota(jnp.int32, (1, 4), 1) == z // 2
    scale = jnp.sum(jnp.where(pick, scales[...].astype(F32), 0.0), axis=1, keepdims=True)
    scaled = (w[...].astype(F32) * scale).astype(BF16)
    sh[0] = scaled[:, :HD]
    sh[1] = scaled[:, HD:]

    pl.semaphore_wait(bar, 2 * NX - 1 + NY - 1 + NZ - 1)

    def x_targets():
        for k in range(NX):
            yield k, (x + k) % NX

    home = x // 2
    for p in range(2):
        def own_place(p=p):
            return W.at[p, z, x % 2, y, pl.ds(pl.multiple_of(c * 16, 16), 16)]

        for k, xx in x_targets():
            cp = remote(sh.at[p], own_place(), ag_x_send.at[p, k], ag_x_recv.at[p], at(xx, y, z, home))
            if k == 0:
                @pl.when(home != c)
                def _():
                    cp.start()

                @pl.when(home == c)
                def _():
                    pltpu.make_async_copy(sh.at[p], own_place(), ag_x_recv.at[p]).start()
            else:
                cp.start()

    for zz in range(NZ):
        remote(tok.at[:, cols(zz, other)], X.at[zz, mine], tok_sem.at[0], tok_sem.at[1], at(x, y, z, other)).start()

    wait_bytes(W.at[0, z, :, y], ag_x_recv.at[0])
    for k in range(1, NY):
        remote(W.at[0, z, :, y], W.at[0, z, :, y], ag_d_send.at[0], ag_d_recv.at[0], at(x, (y + k) % NY, z, c)).start()
    wait_bytes(W.at[1, z, :, y], ag_x_recv.at[1])
    for k in range(1, NZ):
        remote(W.at[1, z, :, y], W.at[1, z, :, y], ag_d_send.at[1], ag_d_recv.at[1], at(x, y, (z + k) % NZ, c)).start()

    wait_bytes(X.at[:, mine], l_sem.at[0])
    wait_bytes(X.at[:, theirs], tok_sem.at[1])

    def turn(zz):
        XT[zz] = X[zz].T

    def piece(p, i, sub):
        if p == 0:
            return W.at[0, i, sub]
        return W.at[1, pl.ds(sub * (NZ // 2), NZ // 2), :, i]

    def ring(p):
        return (z, NZ) if p == 0 else (y, NY)

    def neighbour(p, step):
        if p == 0:
            return at(x, y, (z + step + NZ) % NZ, c)
        return at(x, (y + step + NY) % NY, z, c)

    def ag_copy(p, d, s, sub):
        pos, n = ring(p)
        step = 1 - 2 * d
        i = (pos - step * (s - 1) + n) % n
        return remote(piece(p, i, sub), piece(p, i, sub), ag_send.at[p, d, s - 1, sub], ag_recv.at[p, d, s - 1, sub], neighbour(p, step))

    def ag_arrival(p, d, s, sub):
        pos, n = ring(p)
        step = 1 - 2 * d
        i = (pos - step * s + n) % n
        wait_bytes(piece(p, i, sub), ag_recv.at[p, d, s - 1, sub])

    wait_bytes(W.at[0, pl.ds(0, NY - 1), :, 0], ag_d_recv.at[0])
    for sub in range(2):
        for d in range(2):
            ag_copy(0, d, 1, sub).start()
    wait_bytes(W.at[1, pl.ds(0, NZ - 1), :, 0], ag_d_recv.at[1])
    for sub in range(2):
        for d in range(2):
            ag_copy(1, d, 1, sub).start()
    for s in range(2, 5):
        for zz in range((s - 2) * 3, min((s - 1) * 3, NZ)):
            turn(zz)
        for sub in range(2):
            for p in range(2):
                for d in range(2):
                    ag_arrival(p, d, s - 1, sub)
                    if s < 4 or sub == d:
                        ag_copy(p, d, s, sub).start()
    for p in range(2):
        for d in range(2):
            ag_arrival(p, d, 4, d)

    acc = jnp.zeros((2 * TOK, 2 * HD), F32)
    for zz in range(NZ):
        wz = jnp.concatenate([W[0, zz].reshape(BLK, HD), W[1, zz].reshape(BLK, HD)], axis=1)
        acc += dot(X[zz], wz)
    kvs[...] = acc
    kv_copy = remote(kvs.at[theirs], kvr, kv_sem.at[0], kv_sem.at[1], at(x, y, z, other))
    kv_copy.start()

    seg_t = jnp.broadcast_to(seg[...].astype(F32), (TOK, TOK))
    seg_s = seg_t.T
    s_at = lax.broadcasted_iota(jnp.int32, (TOK, TOK), 0)
    t_at = lax.broadcasted_iota(jnp.int32, (TOK, TOK), 1)
    allowed = (s_at <= t_at) & (seg_s == seg_t)
    q_copy.wait()
    go_copy.wait()

    kv_copy.wait_recv()
    kv = (kvs[mine] + kvr[...]).astype(BF16)
    kb, vb = kv[:, :HD], kv[:, HD:]

    gk = jnp.zeros((TOK, HD), F32)
    gv = jnp.zeros((TOK, HD), F32)
    for h in range(GH):
        qh = qv[:, h * HD:(h + 1) * HD]
        goh = gov[:, h * HD:(h + 1) * HD]
        st = jnp.where(allowed, dot(kb, qh, NT) * SCALE, -1e30)
        top = jnp.max(st, axis=0, keepdims=True)
        ex = jnp.where(allowed, jnp.exp(st - top), 0.0)
        pr = ex * (1.0 / jnp.sum(ex, axis=0, keepdims=True))
        low = pr.astype(BF16)
        plow_s[h] = low
        dp = dot(vb, goh, NT)
        inner = jnp.sum(pr * dp, axis=0, keepdims=True)
        ds = (pr * (dp - inner) * SCALE).astype(BF16)
        gv += dot(low, goh)
        gk += dot(ds, qh)
    G[mine] = jnp.concatenate([gk, gv], axis=1).astype(BF16)
    g_copy = remote(G.at[mine], G.at[mine], g_sem.at[0], g_sem.at[1], at(x, y, z, other))
    g_copy.start()
    wait_bytes(G.at[theirs], g_sem.at[1])

    def partial(p, i):
        if p == 0:
            lhs = XT[i].reshape(BLK, 2 * TOK)
        else:
            lhs = XT.reshape(NZ * 2, NY, 32, 2 * TOK)[:, i].reshape(BLK, 2 * TOK)
        return dot(lhs, G[:, p * HD:(p + 1) * HD])

    H = BLK // 2

    def rs_copy(p, d, s, sub):
        step = 1 - 2 * d
        return remote(
            SB.at[p, d, s - 1, sub], RB.at[p, d, s - 1, sub],
            rs_send.at[p, d, s - 1, sub], rs_recv.at[p, d, s - 1, sub], neighbour(p, step),
        )

    def grad_tokens(zz):
        wz = jnp.concatenate([W[0, zz].reshape(BLK, HD), W[1, zz].reshape(BLK, HD)], axis=1)
        GT[zz] = dot(G[...], wz, NT).astype(BF16)
        pltpu.make_async_copy(GT.at[zz, mine], gtok.at[:, cols(zz, c)], gt_sem.at[0]).start()
        remote(GT.at[zz, theirs], gtok.at[:, cols(zz, c)], gt_sem.at[1], gt_sem.at[2], at(x, y, z, other)).start()

    def attend_out(h):
        attn[:, h * HD:(h + 1) * HD] = dot(plow_s[h], vb, TN).astype(BF16)

    for p in range(2):
        pos, n = ring(p)
        part = partial(p, (pos + 4) % n).astype(BF16)
        for d in range(2):
            SB[p, d, 0, d] = part[d * H:(d + 1) * H]
            rs_copy(p, d, 1, d).start()
    for s in range(2, 5):
        parts = {}
        for p in range(2):
            pos, n = ring(p)
            for d in range(2):
                step = 1 - 2 * d
                parts[p, d] = partial(p, (pos + step * (5 - s) + n) % n)
                if s == 2:
                    sub = 1 - d
                    SB[p, d, s - 1, sub] = parts[p, d][sub * H:(sub + 1) * H].astype(BF16)
                    rs_copy(p, d, s, sub).start()
        for p in range(2):
            for d in range(2):
                for sub in ((d,) if s == 2 else (d, 1 - d)):
                    rs_copy(p, d, s - 1, sub).wait_recv()
                    add = parts[p, d][sub * H:(sub + 1) * H] + RB[p, d, s - 2, sub].astype(F32)
                    SB[p, d, s - 1, sub] = add.astype(BF16)
                    rs_copy(p, d, s, sub).start()
        if s == 2:
            for h in range(GH):
                attend_out(h)
        else:
            for zz in range((s - 3) * 4, (s - 2) * 4):
                grad_tokens(zz)

    for p in range(2):
        pos, n = ring(p)
        own = partial(p, pos)
        for sub in range(2):
            total = own[sub * H:(sub + 1) * H]
            for d in range(2):
                rs_copy(p, d, 4, sub).wait_recv()
                total += RB[p, d, 3, sub].astype(F32)
            if p == 0:
                YS[0, sub] = total.astype(BF16).reshape(NY, 32, HD)
            else:
                YS[1, :, pl.ds(sub * 4, 4)] = total.astype(BF16).reshape(4, 2, 32, HD).transpose(1, 0, 2, 3)
        for k in range(1, 8):
            j = (((y if p == 0 else z)) + k) % 8
            target = at(x, j, z, c) if p == 0 else at(x, y, j, c)
            me = y if p == 0 else z
            remote(YS.at[p, :, j], YR.at[p, :, me], rs_d_send.at[p], rs_d_recv.at[p], target).start()
    for p in range(2):
        me = y if p == 0 else z
        YR[p, :, me] = YS[p, :, me]
        wait_bytes(YR.at[p, :, pl.ds(0, 7)], rs_d_recv.at[p])
        total = jnp.sum(YR[p].astype(F32), axis=1)
        XS[p] = total.astype(BF16)
        for k in range(2):
            for cc in range(2):
                xx = c * 2 + k
                src = XS.at[p, k, pl.ds(cc * 16, 16)]
                dst = XR.at[p, x]

                is_me = (xx == x) & (c == cc)

                @pl.when(is_me)
                def _():
                    pltpu.make_async_copy(src, dst, rs_x_recv.at[p]).start()

                @pl.when(jnp.logical_not(is_me))
                def _():
                    remote(src, dst, rs_x_send.at[p, k, cc], rs_x_recv.at[p], at(xx, y, z, cc)).start()
    for p in range(2):
        wait_bytes(XR.at[p], rs_x_recv.at[p])
        gw[:, p * HD:(p + 1) * HD] = jnp.sum(XR[p].astype(F32), axis=0)

    wait_bytes(gtok.at[:, pl.ds(0, HALF)], gt_sem.at[0])
    wait_bytes(gtok.at[:, pl.ds(0, HALF)], gt_sem.at[1])
    wait_bytes(gtok.at[:, pl.ds(0, HALF)], gt_sem.at[2])
    for p in range(2):
        for k, xx in x_targets():
            cp = remote(sh.at[p], sh.at[p], ag_x_send.at[p, k], ag_x_recv.at[p], at(xx, y, z, home))
            if k == 0:
                @pl.when(home != c)
                def _():
                    cp.wait_send()
            else:
                cp.wait_send()
        wait_bytes(W.at[p, pl.ds(0, 7), :, 0], ag_d_send.at[p])
        wait_bytes(YR.at[p, :, pl.ds(0, 7)], rs_d_send.at[p])
        for d in range(2):
            for s in range(1, 5):
                for sub in range(2):
                    if s < 4 or sub == d:
                        ag_copy(p, d, s, sub).wait_send()
                    if s > 1 or sub == d:
                        rs_copy(p, d, s, sub).wait_send()
        for k in range(2):
            for cc in range(2):
                xx = c * 2 + k
                is_me = (xx == x) & (c == cc)

                @pl.when(jnp.logical_not(is_me))
                def _():
                    remote(XS.at[p, k, pl.ds(cc * 16, 16)], XR.at[p, x], rs_x_send.at[p, k, cc], rs_x_recv.at[p], at(xx, y, z, cc)).wait_send()
    wait_bytes(X.at[:, mine], tok_sem.at[0])
    kv_copy.wait_send()
    g_copy.wait_send()


def shards(tokens, queries, grad_out, seg_ids, w_values, w_scales):
    vmem = pl.BlockSpec(memory_space=pltpu.VMEM)
    hbm = pl.BlockSpec(memory_space=pl.ANY)
    dma = pltpu.SemaphoreType.DMA
    return tuple(pl.pallas_call(
        kernel,
        out_shape=(
            jax.ShapeDtypeStruct((TOK, GH * HD), BF16),
            jax.ShapeDtypeStruct((TOK, D), BF16),
            jax.ShapeDtypeStruct((16, 2 * HD), F32),
        ),
        in_specs=[hbm, hbm, hbm, vmem, vmem, vmem],
        out_specs=(vmem, hbm, vmem),
        scratch_shapes=[
            pltpu.VMEM((NZ, 2 * TOK, BLK), BF16),
            pltpu.VMEM((NZ, BLK, 2 * TOK), BF16),
            pltpu.VMEM((2, NZ, 2, NY, 32, HD), BF16),
            pltpu.VMEM((NZ, 2 * TOK, BLK), BF16),
            pltpu.VMEM((TOK, GH * HD), BF16),
            pltpu.VMEM((TOK, GH * HD), BF16),
            pltpu.VMEM((GH, TOK, TOK), BF16),
            pltpu.VMEM((2, 16, HD), BF16),
            pltpu.VMEM((2 * TOK, 2 * HD), F32),
            pltpu.VMEM((TOK, 2 * HD), F32),
            pltpu.VMEM((2 * TOK, 2 * HD), BF16),
            pltpu.VMEM((2, 2, 4, 2, BLK // 2, HD), BF16),
            pltpu.VMEM((2, 2, 4, 2, BLK // 2, HD), BF16),
            pltpu.VMEM((2, 2, 8, 32, HD), BF16),
            pltpu.VMEM((2, 2, 8, 32, HD), BF16),
            pltpu.VMEM((2, 2, 32, HD), BF16),
            pltpu.VMEM((2, NX, 16, HD), BF16),
            dma((3,)), dma((2,)), dma((2, NX)), dma((2,)), dma((2,)), dma((2,)),
            dma((2, 2, 4, 2)), dma((2, 2, 4, 2)),
            dma((2,)), dma((2,)), dma((3,)),
            dma((2, 2, 4, 2)), dma((2, 2, 4, 2)),
            dma((2,)), dma((2,)), dma((2, 2, 2)), dma((2,)),
        ],
        compiler_params=pltpu.CompilerParams(
            collective_id=0, has_side_effects=True, vmem_limit_bytes=48 * 2**20
        ),
        cost_estimate=pl.CostEstimate(flops=2 * 10**9, bytes_accessed=5 * 2**20, transcendentals=131072),
        name="layer",
    )(tokens, queries, grad_out, seg_ids, w_values, w_scales.reshape(1, 4)))


def solution(mesh):
    spec = P(("node", "dev"), None)
    return jax.shard_map(
        shards,
        mesh=mesh,
        in_specs=(spec, spec, spec, spec, spec, P()),
        out_specs=(spec, spec, spec),
        check_vma=False,
    )
```

```python
import jax
import jax.numpy as jnp
from jax import lax
from jax.experimental import pallas as pl
from jax.experimental.pallas import tpu as pltpu
from jax.sharding import PartitionSpec as P

HD = 128
GH = 8
NX, NY, NZ = 4, 8, 8
TOK = 128
D = 8192
HALF = D // 2
BLK = HALF // NZ
SCALE = HD ** (-0.5)
MESH = pl.DeviceIdType.MESH
F32, BF16 = jnp.float32, jnp.bfloat16
NT = (((1,), (1,)), ((), ()))
TN = (((0,), (0,)), ((), ()))
NN = (((1,), (0,)), ((), ()))
K, V = 0, 1
FAR_X = (2, 1, 3, 0)
FAR = (4, 3, 5, 2, 6, 1, 7, 0)


def dot(a, b, dims=NN):
    return lax.dot_general(a, b, dims, preferred_element_type=F32)


def wait_bytes(ref, sem):
    pltpu.make_async_copy(ref, ref, sem).wait()


def kernel(
    tok, q_hbm, go_hbm, seg, w, scales,
    attn, gtok, gw,
    X, XT, W, GT, qv, gov, prob_s, low_s, sh, kvs, kvr, G, SB, RB, YS, XR,
    l_sem, tok_sem, ag_d_send, ag_d_recv, ag_send, ag_recv,
    kv_sem, g_sem, gt_sem, rs_send, rs_recv, rs_d_send, rs_d_recv,
):
    node, dev = lax.axis_index("node"), lax.axis_index("dev")
    z, x = node // NX, node % NX
    y, c = dev // 2, dev % 2
    other = 1 - c
    home = x // 2

    def at(x, y, z, c):
        return {"node": z * NX + x, "dev": y * 2 + c}

    def remote(src, dst, ss, rs, target):
        return pltpu.make_async_remote_copy(
            src_ref=src, dst_ref=dst, send_sem=ss, recv_sem=rs, device_id=target, device_id_type=MESH
        )

    def cols(zz, core):
        return pl.ds(pl.multiple_of(zz * 2 * BLK + core * BLK, BLK), BLK)

    mine = pl.ds(pl.multiple_of(c * TOK, TOK), TOK)
    theirs = pl.ds(pl.multiple_of(other * TOK, TOK), TOK)

    for zz in range(NZ):
        pltpu.make_async_copy(tok.at[:, cols(zz, c)], X.at[zz, mine], l_sem.at[0]).start()
    q_copy = pltpu.make_async_copy(q_hbm, qv, l_sem.at[1])
    go_copy = pltpu.make_async_copy(go_hbm, gov, l_sem.at[2])
    q_copy.start()
    go_copy.start()

    bar = pltpu.get_barrier_semaphore()

    def greet(device):
        pl.semaphore_signal(bar, inc=1, device_id=device, device_id_type=MESH)

    def gather_target(kx, kk):
        return at((x + kx) % NX, (y + kk * other) % NY, (z + kk * c) % NZ, home)

    def owner(r, xh, kk):
        return at(c * 2 + xh, (y + kk) % NY if r == 0 else y, z if r == 0 else (z + kk) % NZ, r)

    for kk in FAR:
        for kx in FAR_X:
            if kk == 0 and kx == 0:
                @pl.when(home != c)
                def _():
                    greet(gather_target(0, 0))
            else:
                greet(gather_target(kx, kk))
        for r in range(2):
            for xh in range(2):
                if kk == 0:
                    @pl.when(jnp.logical_not((r == c) & (c * 2 + xh == x)))
                    def _():
                        greet(owner(r, xh, 0))
                else:
                    greet(owner(r, xh, kk))
    for step in (1, 7):
        greet(at(x, (y + step) % NY, z, c))
        greet(at(x, y, (z + step) % NZ, c))
    greet(at(x, y, z, other))

    pick = lax.broadcasted_iota(jnp.int32, (1, 4), 1) == z // 2
    scale = jnp.sum(jnp.where(pick, scales[...].astype(F32), 0.0), axis=1, keepdims=True)
    scaled = (w[...].astype(F32) * scale).astype(BF16)
    sh[K] = scaled[:, :HD]
    sh[V] = scaled[:, HD:]

    @pl.when(home == c)
    def _():
        pl.semaphore_wait(bar, 67)

    @pl.when(home != c)
    def _():
        pl.semaphore_wait(bar, 69)

    place = W.at[:, z * 2 + x % 2, y, c]
    for kk in FAR:
        for kx in FAR_X:
            cp = remote(sh, place, ag_d_send, ag_d_recv.at[c], gather_target(kx, kk))
            if kk == 0 and kx == 0:
                @pl.when(home != c)
                def _():
                    cp.start()

                @pl.when(home == c)
                def _():
                    pltpu.make_async_copy(sh, place, ag_d_recv.at[c]).start()
            else:
                cp.start()

    for zz in range(NZ):
        remote(tok.at[:, cols(zz, other)], X.at[zz, mine], tok_sem.at[0], tok_sem.at[1], at(x, y, z, other)).start()

    wait_bytes(X.at[:, mine], l_sem.at[0])
    wait_bytes(X.at[:, theirs], tok_sem.at[1])

    def turn(zz):
        XT[pl.ds(2 * zz, 2)] = X[zz].T.reshape(2, NY, 2, 16, 2 * TOK)

    for zz in range(4):
        turn(zz)

    def piece(p, r, i, sub):
        if r == 0:
            return W.at[p, i * 2 + sub, :, 0]
        return W.at[p, pl.ds(sub * NZ, NZ), i, 1]

    def neighbour(r, step):
        if r == 0:
            return at(x, y, (z + step + NZ) % NZ, c)
        return at(x, (y + step + NY) % NY, z, c)

    pos = (z, y)

    def ag_copy(p, r, d, s, sub):
        step = 1 - 2 * d
        part = piece(p, r, (pos[r] - step * (s - 1) + 8) % 8, sub)
        return remote(part, part, ag_send.at[p], ag_recv.at[p, r, d, s - 1, sub], neighbour(r, step))

    def ag_arrival(p, r, d, s, sub):
        step = 1 - 2 * d
        wait_bytes(piece(p, r, (pos[r] - step * s + 8) % 8, sub), ag_recv.at[p, r, d, s - 1, sub])

    wait_bytes(W.at[:, pl.ds(z * 2, 2), :, 0], ag_d_recv.at[0])
    wait_bytes(W.at[:, :, y, 1], ag_d_recv.at[1])
    streams = ((K, 0), (K, 1), (V, 0), (V, 1))
    for n, (p, sub) in enumerate(streams):
        for r in range(2):
            for d in range(2):
                ag_copy(p, r, d, 1, sub).start()
        turn(4 + n)
    for s in range(2, 5):
        for p, sub in streams:
            for r in range(2):
                for d in range(2):
                    ag_arrival(p, r, d, s - 1, sub)
                    if s < 4 or sub == d:
                        ag_copy(p, r, d, s, sub).start()

    def kv_copy(p):
        return remote(kvs.at[p, theirs], kvr.at[p], kv_sem.at[p], kv_sem.at[2 + p], at(x, y, z, other))

    def rows(p, zz):
        return W[p, pl.ds(2 * zz, 2)].reshape(BLK, HD)

    for p in range(2):
        for r in range(2):
            for sub in range(2):
                ag_arrival(p, r, sub, 4, sub)
        acc = jnp.zeros((2 * TOK, HD), F32)
        for zz in range(NZ):
            acc += dot(X[zz], rows(p, zz))
        kvs[p] = acc
        kv_copy(p).start()

    seg_t = jnp.broadcast_to(seg[...].astype(F32), (TOK, TOK))
    seg_s = seg_t.T
    s_at = lax.broadcasted_iota(jnp.int32, (TOK, TOK), 0)
    t_at = lax.broadcasted_iota(jnp.int32, (TOK, TOK), 1)
    allowed = (s_at <= t_at) & (seg_s == seg_t)
    q_copy.wait()
    go_copy.wait()

    def head(ref, h):
        return ref[:, h * HD:(h + 1) * HD]

    def g_copy(p):
        return remote(G.at[p, mine], G.at[p, mine], g_sem.at[p], g_sem.at[2 + p], at(x, y, z, other))

    kv_copy(K).wait_recv()
    kb = (kvs[K, mine] + kvr[K]).astype(BF16)
    gv = jnp.zeros((TOK, HD), F32)
    for h in range(GH):
        st = jnp.where(allowed, dot(kb, head(qv, h), NT) * SCALE, -1e30)
        top = jnp.max(st, axis=0, keepdims=True)
        ex = jnp.where(allowed, jnp.exp(st - top), 0.0)
        pr = ex * (1.0 / jnp.sum(ex, axis=0, keepdims=True))
        low = pr.astype(BF16)
        prob_s[h] = pr
        low_s[h] = low
        gv += dot(low, head(gov, h))
    G[V, mine] = gv.astype(BF16)
    g_copy(V).start()

    kv_copy(V).wait_recv()
    vb = (kvs[V, mine] + kvr[V]).astype(BF16)
    gk = jnp.zeros((TOK, HD), F32)
    for h in range(GH):
        pr = prob_s[h]
        dp = dot(vb, head(gov, h), NT)
        inner = jnp.sum(pr * dp, axis=0, keepdims=True)
        ds = (pr * (dp - inner) * SCALE).astype(BF16)
        gk += dot(ds, head(qv, h))
    G[K, mine] = gk.astype(BF16)
    g_copy(K).start()

    def partial(p, r, i):
        if r == 0:
            lhs = XT[pl.ds(2 * i, 2), :, 0]
        else:
            lhs = XT[:, i, 1]
        return dot(lhs.reshape(2 * TOK, 2 * TOK), G[p])

    def rs_copy(p, r, d, s, sub):
        return remote(
            SB.at[p, r, d, s - 1, sub], RB.at[p, r, d, s - 1, sub],
            rs_send.at[p], rs_recv.at[p, r, d, s - 1, sub], neighbour(r, 1 - 2 * d),
        )

    def grad_tokens(zz):
        wz = jnp.concatenate([rows(K, zz), rows(V, zz)], axis=1)
        g = jnp.concatenate([G[K], G[V]], axis=1)
        GT[zz] = dot(g, wz, NT).astype(BF16)
        pltpu.make_async_copy(GT.at[zz, mine], gtok.at[:, cols(zz, c)], gt_sem.at[0]).start()
        remote(GT.at[zz, theirs], gtok.at[:, cols(zz, c)], gt_sem.at[1], gt_sem.at[2], at(x, y, z, other)).start()

    def attend_out(h):
        attn[:, h * HD:(h + 1) * HD] = dot(low_s[h], vb, TN).astype(BF16)

    H = TOK
    for p in (V, K):
        wait_bytes(G.at[p, theirs], g_sem.at[2 + p])
        for r in range(2):
            part = partial(p, r, (pos[r] + 4) % 8).astype(BF16)
            for d in range(2):
                SB[p, r, d, 0, d] = part[d * H:(d + 1) * H]
                rs_copy(p, r, d, 1, d).start()
    for s in range(2, 5):
        for p in (V, K):
            parts = {}
            for r in range(2):
                for d in range(2):
                    step = 1 - 2 * d
                    parts[r, d] = partial(p, r, (pos[r] + step * (5 - s) + 8) % 8)
                    if s == 2:
                        sub = 1 - d
                        SB[p, r, d, s - 1, sub] = parts[r, d][sub * H:(sub + 1) * H].astype(BF16)
                        rs_copy(p, r, d, s, sub).start()
            for sub in range(2):
                for r in range(2):
                    for d in range(2):
                        if s == 2 and sub != d:
                            continue
                        rs_copy(p, r, d, s - 1, sub).wait_recv()
                        add = parts[r, d][sub * H:(sub + 1) * H] + RB[p, r, d, s - 2, sub].astype(F32)
                        SB[p, r, d, s - 1, sub] = add.astype(BF16)
                        rs_copy(p, r, d, s, sub).start()
            half = 0 if p == V else 1
            if s == 2:
                for h in range(half * 4, half * 4 + 4):
                    attend_out(h)
            else:
                for zz in range((s - 3) * 4 + half * 2, (s - 3) * 4 + half * 2 + 2):
                    grad_tokens(zz)

    for p in (V, K):
        for r in range(2):
            own = partial(p, r, pos[r])
            for sub in range(2):
                total = own[sub * H:(sub + 1) * H]
                for d in range(2):
                    rs_copy(p, r, d, 4, sub).wait_recv()
                    total += RB[p, r, d, 3, sub].astype(F32)
                YS[r, pl.ds(sub * 8, 8), p] = total.astype(BF16).reshape(8, 16, HD)
    for kk in FAR:
        for r in range(2):
            for xh in range(2):
                if r == 0:
                    src = YS.at[0, xh * 8 + (y + kk) % NY]
                    dst = XR.at[x * 8 + y]
                else:
                    src = YS.at[1, (z + kk) % NZ * 2 + xh]
                    dst = XR.at[x * 8 + z]
                cp = remote(src, dst, rs_d_send, rs_d_recv, owner(r, xh, kk))
                if kk == 0:
                    is_me = (r == c) & (c * 2 + xh == x)

                    @pl.when(jnp.logical_not(is_me))
                    def _():
                        cp.start()

                    @pl.when(is_me)
                    def _():
                        pltpu.make_async_copy(src, dst, rs_d_recv).start()
                else:
                    cp.start()

    for k in range(3):
        wait_bytes(gtok.at[:, pl.ds(0, HALF)], gt_sem.at[k])
    for p in range(2):
        wait_bytes(W.at[p, pl.ds(0, 14)], ag_send.at[p])
        wait_bytes(W.at[p, pl.ds(0, 14)], rs_send.at[p])
        kv_copy(p).wait_send()
        g_copy(p).wait_send()
    wait_bytes(X.at[:, mine], tok_sem.at[0])

    @pl.when(home == c)
    def _():
        wait_bytes(XR.at[pl.ds(0, 31)], ag_d_send)

    @pl.when(home != c)
    def _():
        wait_bytes(XR, ag_d_send)

    wait_bytes(XR, rs_d_recv)
    for p in range(2):
        gw[:, p * HD:(p + 1) * HD] = jnp.sum(XR[:, p].astype(F32), axis=0)

    @pl.when(home == c)
    def _():
        wait_bytes(XR.at[pl.ds(0, 31)], rs_d_send)

    @pl.when(home != c)
    def _():
        wait_bytes(XR, rs_d_send)


def shards(tokens, queries, grad_out, seg_ids, w_values, w_scales):
    vmem = pl.BlockSpec(memory_space=pltpu.VMEM)
    hbm = pl.BlockSpec(memory_space=pl.ANY)
    dma = pltpu.SemaphoreType.DMA
    return tuple(pl.pallas_call(
        kernel,
        out_shape=(
            jax.ShapeDtypeStruct((TOK, GH * HD), BF16),
            jax.ShapeDtypeStruct((TOK, D), BF16),
            jax.ShapeDtypeStruct((16, 2 * HD), F32),
        ),
        in_specs=[hbm, hbm, hbm, vmem, vmem, vmem],
        out_specs=(vmem, hbm, vmem),
        scratch_shapes=[
            pltpu.VMEM((NZ, 2 * TOK, BLK), BF16),
            pltpu.VMEM((2 * NZ, NY, 2, 16, 2 * TOK), BF16),
            pltpu.VMEM((2, 2 * NZ, NY, 2, 16, HD), BF16),
            pltpu.VMEM((NZ, 2 * TOK, BLK), BF16),
            pltpu.VMEM((TOK, GH * HD), BF16),
            pltpu.VMEM((TOK, GH * HD), BF16),
            pltpu.VMEM((GH, TOK, TOK), F32),
            pltpu.VMEM((GH, TOK, TOK), BF16),
            pltpu.VMEM((2, 16, HD), BF16),
            pltpu.VMEM((2, 2 * TOK, HD), F32),
            pltpu.VMEM((2, TOK, HD), F32),
            pltpu.VMEM((2, 2 * TOK, HD), BF16),
            pltpu.VMEM((2, 2, 2, 4, 2, TOK, HD), BF16),
            pltpu.VMEM((2, 2, 2, 4, 2, TOK, HD), BF16),
            pltpu.VMEM((2, 16, 2, 16, HD), BF16),
            pltpu.VMEM((32, 2, 16, HD), BF16),
            dma((3,)), dma((2,)), dma, dma((2,)), dma((2,)), dma((2, 2, 2, 4, 2)),
            dma((4,)), dma((4,)), dma((3,)), dma((2,)), dma((2, 2, 2, 4, 2)), dma, dma,
        ],
        compiler_params=pltpu.CompilerParams(
            collective_id=0, has_side_effects=True, vmem_limit_bytes=60 * 2**20
        ),
        cost_estimate=pl.CostEstimate(flops=2 * 10**9, bytes_accessed=5 * 2**20, transcendentals=131072),
        name="layer",
    )(tokens, queries, grad_out, seg_ids, w_values, w_scales.reshape(1, 4)))


def solution(mesh):
    spec = P(("node", "dev"), None)
    return jax.shard_map(
        shards,
        mesh=mesh,
        in_specs=(spec, spec, spec, spec, spec, P()),
        out_specs=(spec, spec, spec),
        check_vma=False,
    )
```

```python
import jax
import jax.numpy as jnp
from jax import lax
from jax.experimental import pallas as pl
from jax.experimental.pallas import tpu as pltpu
from jax.sharding import PartitionSpec as P

HD = 128
GH = 8
NX, NY, NZ = 4, 8, 8
TOK = 128
D = 8192
HALF = D // 2
BLK = HALF // NZ
SCALE = HD ** (-0.5)
MESH = pl.DeviceIdType.MESH
F32, BF16 = jnp.float32, jnp.bfloat16
NT = (((1,), (1,)), ((), ()))
TN = (((0,), (0,)), ((), ()))
NN = (((1,), (0,)), ((), ()))
K, V = 0, 1
FAR_X = (2, 1, 3, 0)
FAR = (4, 3, 5, 2, 6, 1, 7, 0)


def dot(a, b, dims=NN):
    return lax.dot_general(a, b, dims, preferred_element_type=F32)


def wait_bytes(ref, sem):
    pltpu.make_async_copy(ref, ref, sem).wait()


def kernel(
    tok, q_hbm, go_hbm, seg_hbm, w_hbm, scales_hbm,
    attn, gtok, gw,
    seg, w, scales, X, XT, W, GT, qv, gov, prob_s, low_s, sh, kvs, kvr, G, SB, RB, YS, XR,
    l_sem, tok_sem, ag_d_send, ag_d_recv, ag_send, ag_recv,
    kv_sem, g_sem, gt_sem, rs_send, rs_recv, rs_d_send, rs_d_recv,
):
    node, dev = lax.axis_index("node"), lax.axis_index("dev")
    z, x = node // NX, node % NX
    y, c = dev // 2, dev % 2
    other = 1 - c
    home = x // 2

    def at(x, y, z, c):
        return {"node": z * NX + x, "dev": y * 2 + c}

    def remote(src, dst, ss, rs, target):
        return pltpu.make_async_remote_copy(
            src_ref=src, dst_ref=dst, send_sem=ss, recv_sem=rs, device_id=target, device_id_type=MESH
        )

    def cols(zz, core):
        return pl.ds(pl.multiple_of(zz * 2 * BLK + core * BLK, BLK), BLK)

    mine = pl.ds(pl.multiple_of(c * TOK, TOK), TOK)
    theirs = pl.ds(pl.multiple_of(other * TOK, TOK), TOK)

    bar = pltpu.get_barrier_semaphore()

    def greet(device):
        pl.semaphore_signal(bar, inc=1, device_id=device, device_id_type=MESH)

    def gather_target(kx, kk):
        return at((x + kx) % NX, (y + kk * other) % NY, (z + kk * c) % NZ, home)

    def owner(r, xh, kk):
        return at(c * 2 + xh, (y + kk) % NY if r == 0 else y, z if r == 0 else (z + kk) % NZ, r)

    for kk in FAR:
        for kx in FAR_X:
            if kk == 0 and kx == 0:
                @pl.when(home != c)
                def _():
                    greet(gather_target(0, 0))
            else:
                greet(gather_target(kx, kk))
        for r in range(2):
            for xh in range(2):
                if kk == 0:
                    @pl.when(jnp.logical_not((r == c) & (c * 2 + xh == x)))
                    def _():
                        greet(owner(r, xh, 0))
                else:
                    greet(owner(r, xh, kk))
    for step in (1, 7):
        greet(at(x, (y + step) % NY, z, c))
        greet(at(x, y, (z + step) % NZ, c))
    greet(at(x, y, z, other))

    small = [
        pltpu.make_async_copy(src, dst, l_sem.at[3 + n])
        for n, (src, dst) in enumerate(((w_hbm, w), (scales_hbm, scales), (seg_hbm, seg)))
    ]
    for copy in small:
        copy.start()
    for zz in range(NZ):
        pltpu.make_async_copy(tok.at[:, cols(zz, c)], X.at[zz, mine], l_sem.at[0]).start()
    q_copy = pltpu.make_async_copy(q_hbm, qv, l_sem.at[1])
    go_copy = pltpu.make_async_copy(go_hbm, gov, l_sem.at[2])
    q_copy.start()
    go_copy.start()

    small[0].wait()
    small[1].wait()
    pick = lax.broadcasted_iota(jnp.int32, (1, 4), 1) == z // 2
    scale = jnp.sum(jnp.where(pick, scales[...].astype(F32), 0.0), axis=1, keepdims=True)
    scaled = (w[...].astype(F32) * scale).astype(BF16)
    sh[K] = scaled[:, :HD]
    sh[V] = scaled[:, HD:]

    @pl.when(home == c)
    def _():
        pl.semaphore_wait(bar, 67)

    @pl.when(home != c)
    def _():
        pl.semaphore_wait(bar, 69)

    place = W.at[:, z * 2 + x % 2, y, c]
    for kk in FAR:
        for kx in FAR_X:
            cp = remote(sh, place, ag_d_send, ag_d_recv.at[c], gather_target(kx, kk))
            if kk == 0 and kx == 0:
                @pl.when(home != c)
                def _():
                    cp.start()

                @pl.when(home == c)
                def _():
                    pltpu.make_async_copy(sh, place, ag_d_recv.at[c]).start()
            else:
                cp.start()

    for zz in range(NZ):
        remote(tok.at[:, cols(zz, other)], X.at[zz, mine], tok_sem.at[0], tok_sem.at[1], at(x, y, z, other)).start()

    wait_bytes(X.at[:, mine], l_sem.at[0])
    wait_bytes(X.at[:, theirs], tok_sem.at[1])

    def turn(zz):
        XT[pl.ds(2 * zz, 2)] = X[zz].T.reshape(2, NY, 2, 16, 2 * TOK)

    for zz in range(4):
        turn(zz)

    def piece(p, r, i, sub):
        if r == 0:
            return W.at[p, i * 2 + sub, :, 0]
        return W.at[p, pl.ds(sub * NZ, NZ), i, 1]

    def neighbour(r, step):
        if r == 0:
            return at(x, y, (z + step + NZ) % NZ, c)
        return at(x, (y + step + NY) % NY, z, c)

    pos = (z, y)

    def ag_copy(p, r, d, s, sub):
        step = 1 - 2 * d
        part = piece(p, r, (pos[r] - step * (s - 1) + 8) % 8, sub)
        return remote(part, part, ag_send.at[p], ag_recv.at[p, r, d, s - 1, sub], neighbour(r, step))

    def ag_arrival(p, r, d, s, sub):
        step = 1 - 2 * d
        wait_bytes(piece(p, r, (pos[r] - step * s + 8) % 8, sub), ag_recv.at[p, r, d, s - 1, sub])

    wait_bytes(W.at[:, pl.ds(z * 2, 2), :, 0], ag_d_recv.at[0])
    wait_bytes(W.at[:, :, y, 1], ag_d_recv.at[1])
    streams = ((K, 0), (K, 1), (V, 0), (V, 1))
    for n, (p, sub) in enumerate(streams):
        for r in range(2):
            for d in range(2):
                ag_copy(p, r, d, 1, sub).start()
        turn(4 + n)
    for s in range(2, 5):
        for p, sub in streams:
            for r in range(2):
                for d in range(2):
                    ag_arrival(p, r, d, s - 1, sub)
                    if s < 4 or sub == d:
                        ag_copy(p, r, d, s, sub).start()

    def kv_copy(p):
        return remote(kvs.at[p, theirs], kvr.at[p], kv_sem.at[p], kv_sem.at[2 + p], at(x, y, z, other))

    def rows(p, zz):
        return W[p, pl.ds(2 * zz, 2)].reshape(BLK, HD)

    for p in range(2):
        for r in range(2):
            for sub in range(2):
                ag_arrival(p, r, sub, 4, sub)
        acc = jnp.zeros((2 * TOK, HD), F32)
        for zz in range(NZ):
            acc += dot(X[zz], rows(p, zz))
        kvs[p] = acc
        kv_copy(p).start()

    small[2].wait()
    seg_t = jnp.broadcast_to(seg[...].astype(F32), (TOK, TOK))
    seg_s = seg_t.T
    s_at = lax.broadcasted_iota(jnp.int32, (TOK, TOK), 0)
    t_at = lax.broadcasted_iota(jnp.int32, (TOK, TOK), 1)
    one = jnp.where((s_at <= t_at) & (seg_s == seg_t), 1.0, 0.0)
    allowed = jnp.concatenate([one, one], axis=1) > 0.5
    q_copy.wait()
    go_copy.wait()

    def pair(ref, h):
        return jnp.concatenate([ref[:, h * HD:(h + 1) * HD], ref[:, (h + 1) * HD:(h + 2) * HD]], axis=0)

    def g_copy(p):
        return remote(G.at[p, mine], G.at[p, mine], g_sem.at[p], g_sem.at[2 + p], at(x, y, z, other))

    kv_copy(K).wait_recv()
    kb = (kvs[K, mine] + kvr[K]).astype(BF16)
    gv = jnp.zeros((TOK, HD), F32)
    for h in range(0, GH, 2):
        st = jnp.where(allowed, dot(kb, pair(qv, h), NT) * SCALE, -1e30)
        top = jnp.max(st, axis=0, keepdims=True)
        ex = jnp.where(allowed, jnp.exp(st - top), 0.0)
        pr = ex * (1.0 / jnp.sum(ex, axis=0, keepdims=True))
        low = pr.astype(BF16)
        prob_s[h // 2] = pr
        low_s[h // 2] = low
        gv += dot(low, pair(gov, h))
    G[V, mine] = gv.astype(BF16)
    g_copy(V).start()

    kv_copy(V).wait_recv()
    vb = (kvs[V, mine] + kvr[V]).astype(BF16)
    gk = jnp.zeros((TOK, HD), F32)
    for h in range(0, GH, 2):
        pr = prob_s[h // 2]
        dp = dot(vb, pair(gov, h), NT)
        inner = jnp.sum(pr * dp, axis=0, keepdims=True)
        ds = (pr * (dp - inner) * SCALE).astype(BF16)
        gk += dot(ds, pair(qv, h))
    G[K, mine] = gk.astype(BF16)
    g_copy(K).start()

    def partial(p, r, i):
        if r == 0:
            lhs = XT[pl.ds(2 * i, 2), :, 0]
        else:
            lhs = XT[:, i, 1]
        return dot(lhs.reshape(2 * TOK, 2 * TOK), G[p])

    def rs_copy(p, r, d, s, sub):
        return remote(
            SB.at[p, r, d, s - 1, sub], RB.at[p, r, d, s - 1, sub],
            rs_send.at[p], rs_recv.at[p, r, d, s - 1, sub], neighbour(r, 1 - 2 * d),
        )

    def grad_tokens(zz):
        wz = jnp.concatenate([rows(K, zz), rows(V, zz)], axis=1)
        g = jnp.concatenate([G[K], G[V]], axis=1)
        GT[zz] = dot(g, wz, NT).astype(BF16)
        gtok[:, cols(zz, c)] = GT[zz, mine]
        remote(GT.at[zz, theirs], gtok.at[:, cols(zz, c)], gt_sem.at[0], gt_sem.at[1], at(x, y, z, other)).start()

    def attend_out(h):
        attn[:, h * HD:(h + 1) * HD] = dot(low_s[h // 2, :, h % 2 * TOK:(h % 2 + 1) * TOK], vb, TN).astype(BF16)

    H = TOK
    for p in (V, K):
        wait_bytes(G.at[p, theirs], g_sem.at[2 + p])
        for r in range(2):
            part = partial(p, r, (pos[r] + 4) % 8).astype(BF16)
            for d in range(2):
                SB[p, r, d, 0, d] = part[d * H:(d + 1) * H]
                rs_copy(p, r, d, 1, d).start()
    for s in range(2, 5):
        for p in (V, K):
            parts = {}
            for r in range(2):
                for d in range(2):
                    step = 1 - 2 * d
                    parts[r, d] = partial(p, r, (pos[r] + step * (5 - s) + 8) % 8)
                    if s == 2:
                        sub = 1 - d
                        SB[p, r, d, s - 1, sub] = parts[r, d][sub * H:(sub + 1) * H].astype(BF16)
                        rs_copy(p, r, d, s, sub).start()
            for sub in range(2):
                for r in range(2):
                    for d in range(2):
                        if s == 2 and sub != d:
                            continue
                        rs_copy(p, r, d, s - 1, sub).wait_recv()
                        add = parts[r, d][sub * H:(sub + 1) * H] + RB[p, r, d, s - 2, sub].astype(F32)
                        SB[p, r, d, s - 1, sub] = add.astype(BF16)
                        rs_copy(p, r, d, s, sub).start()
            half = 0 if p == V else 1
            if s == 2:
                for h in range(half * 4, half * 4 + 4):
                    attend_out(h)
            else:
                for zz in range((s - 3) * 4 + half * 2, (s - 3) * 4 + half * 2 + 2):
                    grad_tokens(zz)

    for p in (V, K):
        for r in range(2):
            own = partial(p, r, pos[r])
            for sub in range(2):
                total = own[sub * H:(sub + 1) * H]
                for d in range(2):
                    rs_copy(p, r, d, 4, sub).wait_recv()
                    total += RB[p, r, d, 3, sub].astype(F32)
                YS[r, pl.ds(sub * 8, 8), p] = total.astype(BF16).reshape(8, 16, HD)
    for kk in FAR:
        for r in range(2):
            for xh in range(2):
                if r == 0:
                    src = YS.at[0, xh * 8 + (y + kk) % NY]
                    dst = XR.at[x * 8 + y]
                else:
                    src = YS.at[1, (z + kk) % NZ * 2 + xh]
                    dst = XR.at[x * 8 + z]
                cp = remote(src, dst, rs_d_send, rs_d_recv, owner(r, xh, kk))
                if kk == 0:
                    is_me = (r == c) & (c * 2 + xh == x)

                    @pl.when(jnp.logical_not(is_me))
                    def _():
                        cp.start()

                    @pl.when(is_me)
                    def _():
                        pltpu.make_async_copy(src, dst, rs_d_recv).start()
                else:
                    cp.start()

    for k in range(2):
        wait_bytes(gtok.at[:, pl.ds(0, HALF)], gt_sem.at[k])
    for p in range(2):
        wait_bytes(W.at[p, pl.ds(0, 14)], ag_send.at[p])
        wait_bytes(W.at[p, pl.ds(0, 14)], rs_send.at[p])
        kv_copy(p).wait_send()
        g_copy(p).wait_send()
    wait_bytes(X.at[:, mine], tok_sem.at[0])

    @pl.when(home == c)
    def _():
        wait_bytes(XR.at[pl.ds(0, 31)], ag_d_send)

    @pl.when(home != c)
    def _():
        wait_bytes(XR, ag_d_send)

    wait_bytes(XR, rs_d_recv)
    for p in range(2):
        gw[:, p * HD:(p + 1) * HD] = jnp.sum(XR[:, p].astype(F32), axis=0)

    @pl.when(home == c)
    def _():
        wait_bytes(XR.at[pl.ds(0, 31)], rs_d_send)

    @pl.when(home != c)
    def _():
        wait_bytes(XR, rs_d_send)


OUTS = (((TOK, GH * HD), BF16), ((TOK, D), BF16), ((16, 2 * HD), F32))


def write_out(*refs):
    copies = [pltpu.make_async_copy(refs[i], refs[3 + i], refs[6].at[i]) for i in range(3)]
    for copy in copies:
        copy.start()
    for copy in copies:
        copy.wait()


def shards(tokens, queries, grad_out, seg_ids, w_values, w_scales):
    vmem = pl.BlockSpec(memory_space=pltpu.VMEM)
    hbm = pl.BlockSpec(memory_space=pltpu.HBM)
    dma = pltpu.SemaphoreType.DMA
    inner = pl.pallas_call(
        kernel,
        out_shape=tuple(pltpu.VMEM(shape, dtype) for shape, dtype in OUTS),
        in_specs=[hbm] * 6,
        out_specs=(vmem, vmem, vmem),
        scratch_shapes=[
            pltpu.VMEM((1, TOK), jnp.int32),
            pltpu.VMEM((16, 2 * HD), BF16),
            pltpu.VMEM((1, 4), BF16),
            pltpu.VMEM((NZ, 2 * TOK, BLK), BF16),
            pltpu.VMEM((2 * NZ, NY, 2, 16, 2 * TOK), BF16),
            pltpu.VMEM((2, 2 * NZ, NY, 2, 16, HD), BF16),
            pltpu.VMEM((NZ, 2 * TOK, BLK), BF16),
            pltpu.VMEM((TOK, GH * HD), BF16),
            pltpu.VMEM((TOK, GH * HD), BF16),
            pltpu.VMEM((GH // 2, TOK, 2 * TOK), F32),
            pltpu.VMEM((GH // 2, TOK, 2 * TOK), BF16),
            pltpu.VMEM((2, 16, HD), BF16),
            pltpu.VMEM((2, 2 * TOK, HD), F32),
            pltpu.VMEM((2, TOK, HD), F32),
            pltpu.VMEM((2, 2 * TOK, HD), BF16),
            pltpu.VMEM((2, 2, 2, 4, 2, TOK, HD), BF16),
            pltpu.VMEM((2, 2, 2, 4, 2, TOK, HD), BF16),
            pltpu.VMEM((2, 16, 2, 16, HD), BF16),
            pltpu.VMEM((32, 2, 16, HD), BF16),
            dma((6,)), dma((2,)), dma, dma((2,)), dma((2,)), dma((2, 2, 2, 4, 2)),
            dma((4,)), dma((4,)), dma((2,)), dma((2,)), dma((2, 2, 2, 4, 2)), dma, dma,
        ],
        compiler_params=pltpu.CompilerParams(
            collective_id=0, has_side_effects=True, vmem_limit_bytes=60 * 2**20
        ),
        cost_estimate=pl.CostEstimate(flops=2 * 10**9, bytes_accessed=5 * 2**20, transcendentals=131072),
        name="layer",
    )(tokens, queries, grad_out, seg_ids, w_values, w_scales.reshape(1, 4))
    return tuple(pl.pallas_call(
        write_out,
        out_shape=tuple(jax.ShapeDtypeStruct(shape, dtype) for shape, dtype in OUTS),
        in_specs=[vmem] * 3,
        out_specs=(pl.BlockSpec(memory_space=pl.ANY),) * 3,
        scratch_shapes=[dma((3,))],
        name="write_out",
    )(*inner))


def solution(mesh):
    spec = P(("node", "dev"), None)
    return jax.shard_map(
        shards,
        mesh=mesh,
        in_specs=(spec, spec, spec, spec, spec, P()),
        out_specs=(spec, spec, spec),
        check_vma=False,
    )
```

```python
import jax
import jax.numpy as jnp
from jax import lax
from jax.experimental import pallas as pl
from jax.experimental.pallas import tpu as pltpu
from jax.sharding import PartitionSpec as P

HD = 128
GH = 8
NX, NY, NZ = 4, 8, 8
TOK = 128
D = 8192
HALF = D // 2
BLK = HALF // NZ
SCALE = HD ** (-0.5)
MESH = pl.DeviceIdType.MESH
F32, BF16 = jnp.float32, jnp.bfloat16
NT = (((1,), (1,)), ((), ()))
TN = (((0,), (0,)), ((), ()))
NN = (((1,), (0,)), ((), ()))
K, V = 0, 1
FAR_X = (2, 1, 3, 0)
FAR = (4, 3, 5, 2, 6, 1, 7, 0)


def dot(a, b, dims=NN):
    return lax.dot_general(a, b, dims, preferred_element_type=F32)


def wait_bytes(ref, sem):
    pltpu.make_async_copy(ref, ref, sem).wait()


def kernel(
    tok, q_hbm, go_hbm, seg_hbm, w_hbm, scales_hbm,
    attn, gtok, gw,
    seg, w, scales, X, XT, W, GT, qv, gov, prob_s, low_s, sh, kvs, kvr, G, SB, RB, YS, XR,
    l_sem, tok_sem, ag_d_send, ag_d_recv, ag_send, ag_recv,
    kv_sem, g_sem, gt_sem, rs_send, rs_recv, rs_d_send, rs_d_recv,
):
    node, dev = lax.axis_index("node"), lax.axis_index("dev")
    z, x = node // NX, node % NX
    y, c = dev // 2, dev % 2
    other = 1 - c
    home = x // 2

    def at(x, y, z, c):
        return {"node": z * NX + x, "dev": y * 2 + c}

    def remote(src, dst, ss, rs, target):
        return pltpu.make_async_remote_copy(
            src_ref=src, dst_ref=dst, send_sem=ss, recv_sem=rs, device_id=target, device_id_type=MESH
        )

    def cols(zz, core):
        return pl.ds(pl.multiple_of(zz * 2 * BLK + core * BLK, BLK), BLK)

    mine = pl.ds(pl.multiple_of(c * TOK, TOK), TOK)
    theirs = pl.ds(pl.multiple_of(other * TOK, TOK), TOK)

    bar = pltpu.get_barrier_semaphore()

    def greet(device):
        pl.semaphore_signal(bar, inc=1, device_id=device, device_id_type=MESH)

    def gather_target(kx, kk):
        return at((x + kx) % NX, (y + kk * other) % NY, (z + kk * c) % NZ, home)

    def owner(r, xh, kk):
        return at(c * 2 + xh, (y + kk) % NY if r == 0 else y, z if r == 0 else (z + kk) % NZ, r)

    for kk in FAR:
        for kx in FAR_X:
            if kk == 0 and kx == 0:
                @pl.when(home != c)
                def _():
                    greet(gather_target(0, 0))
            else:
                greet(gather_target(kx, kk))
        for r in range(2):
            for xh in range(2):
                if kk == 0:
                    @pl.when(jnp.logical_not((r == c) & (c * 2 + xh == x)))
                    def _():
                        greet(owner(r, xh, 0))
                else:
                    greet(owner(r, xh, kk))
    for step in (1, 2, 6, 7):
        greet(at(x, (y + step) % NY, z, c))
        greet(at(x, y, (z + step) % NZ, c))
    greet(at(x, y, z, other))

    small = [
        pltpu.make_async_copy(src, dst, l_sem.at[3 + n])
        for n, (src, dst) in enumerate(((w_hbm, w), (scales_hbm, scales), (seg_hbm, seg)))
    ]
    for copy in small:
        copy.start()
    for zz in range(NZ):
        pltpu.make_async_copy(tok.at[:, cols(zz, c)], X.at[zz, mine], l_sem.at[0]).start()
    q_copy = pltpu.make_async_copy(q_hbm, qv, l_sem.at[1])
    go_copy = pltpu.make_async_copy(go_hbm, gov, l_sem.at[2])
    q_copy.start()
    go_copy.start()

    small[0].wait()
    small[1].wait()
    pick = lax.broadcasted_iota(jnp.int32, (1, 4), 1) == z // 2
    scale = jnp.sum(jnp.where(pick, scales[...].astype(F32), 0.0), axis=1, keepdims=True)
    scaled = (w[...].astype(F32) * scale).astype(BF16)
    sh[K] = scaled[:, :HD]
    sh[V] = scaled[:, HD:]

    @pl.when(home == c)
    def _():
        pl.semaphore_wait(bar, 71)

    @pl.when(home != c)
    def _():
        pl.semaphore_wait(bar, 73)

    place = W.at[:, z * 2 + x % 2, y, c]
    for kk in FAR:
        for kx in FAR_X:
            cp = remote(sh, place, ag_d_send, ag_d_recv.at[c], gather_target(kx, kk))
            if kk == 0 and kx == 0:
                @pl.when(home != c)
                def _():
                    cp.start()

                @pl.when(home == c)
                def _():
                    pltpu.make_async_copy(sh, place, ag_d_recv.at[c]).start()
            else:
                cp.start()

    for zz in range(NZ):
        remote(tok.at[:, cols(zz, other)], X.at[zz, mine], tok_sem.at[0], tok_sem.at[1], at(x, y, z, other)).start()

    wait_bytes(X.at[:, mine], l_sem.at[0])
    wait_bytes(X.at[:, theirs], tok_sem.at[1])

    def turn(zz):
        XT[pl.ds(2 * zz, 2)] = X[zz].T.reshape(2, NY, 2, 16, 2 * TOK)

    for zz in range(4):
        turn(zz)

    def piece(p, r, i, sub):
        if r == 0:
            return W.at[p, i * 2 + sub, :, 0]
        return W.at[p, pl.ds(sub * NZ, NZ), i, 1]

    def neighbour(r, step):
        if r == 0:
            return at(x, y, (z + step + NZ) % NZ, c)
        return at(x, (y + step + NY) % NY, z, c)

    pos = (z, y)

    def ag_copy(p, r, d, k, places, sub):
        step = 1 - 2 * d
        part = piece(p, r, (pos[r] - step * k + 8) % 8, sub)
        return remote(part, part, ag_send.at[p], ag_recv.at[p, r, d, k + places - 1, sub], neighbour(r, step * places))

    def ag_arrival(p, r, d, k, sub):
        wait_bytes(piece(p, r, (pos[r] - (1 - 2 * d) * k + 8) % 8, sub), ag_recv.at[p, r, d, k - 1, sub])

    GOES = ({0: (2, 1), 2: (2, 1)}, {0: (1,), 1: (1,), 2: (2, 1)})

    def ag_pass(p, k):
        for sub in range(2):
            for r in range(2):
                for d in range(2):
                    if k == 4 and sub != d:
                        continue
                    if k > 0:
                        ag_arrival(p, r, d, k, sub)
                    for places in GOES[p].get(k, ()):
                        if k + places < 4 or sub == d:
                            ag_copy(p, r, d, k, places, sub).start()

    wait_bytes(W.at[:, pl.ds(z * 2, 2), :, 0], ag_d_recv.at[0])
    wait_bytes(W.at[:, :, y, 1], ag_d_recv.at[1])
    ag_pass(K, 0)
    ag_pass(V, 0)
    for zz in range(4, 6):
        turn(zz)
    ag_pass(K, 2)
    ag_pass(V, 1)
    for zz in range(6, 8):
        turn(zz)
    ag_pass(K, 1)
    ag_pass(V, 2)

    def kv_copy(p):
        return remote(kvs.at[p, theirs], kvr.at[p], kv_sem.at[p], kv_sem.at[2 + p], at(x, y, z, other))

    def rows(p, zz):
        return W[p, pl.ds(2 * zz, 2)].reshape(BLK, HD)

    def project(p):
        ag_pass(p, 3)
        ag_pass(p, 4)
        acc = jnp.zeros((2 * TOK, HD), F32)
        for zz in range(NZ):
            acc += dot(X[zz], rows(p, zz))
        kvs[p] = acc
        kv_copy(p).start()

    project(K)
    small[2].wait()
    seg_t = jnp.broadcast_to(seg[...].astype(F32), (TOK, TOK))
    seg_s = seg_t.T
    s_at = lax.broadcasted_iota(jnp.int32, (TOK, TOK), 0)
    t_at = lax.broadcasted_iota(jnp.int32, (TOK, TOK), 1)
    one = jnp.where((s_at <= t_at) & (seg_s == seg_t), 1.0, 0.0)
    allowed = jnp.concatenate([one, one], axis=1) > 0.5
    q_copy.wait()
    go_copy.wait()

    def pair(ref, h):
        return jnp.concatenate([ref[:, h * HD:(h + 1) * HD], ref[:, (h + 1) * HD:(h + 2) * HD]], axis=0)

    def g_copy(p):
        return remote(G.at[p, mine], G.at[p, mine], g_sem.at[p], g_sem.at[2 + p], at(x, y, z, other))

    kv_copy(K).wait_recv()
    kb = (kvs[K, mine] + kvr[K]).astype(BF16)
    gv = jnp.zeros((TOK, HD), F32)
    for h in range(0, GH, 2):
        st = jnp.where(allowed, dot(kb, pair(qv, h), NT) * SCALE, -1e30)
        top = jnp.max(st, axis=0, keepdims=True)
        ex = jnp.where(allowed, jnp.exp(st - top), 0.0)
        pr = ex * (1.0 / jnp.sum(ex, axis=0, keepdims=True))
        low = pr.astype(BF16)
        prob_s[h // 2] = pr
        low_s[h // 2] = low
        gv += dot(low, pair(gov, h))
    G[V, mine] = gv.astype(BF16)
    g_copy(V).start()

    project(V)

    H = TOK

    def partial(p, r, places):
        i = (pos[r] + places + 8) % 8
        if r == 0:
            lhs = XT[pl.ds(2 * i, 2), :, 0]
        else:
            lhs = XT[:, i, 1]
        return dot(lhs.reshape(2 * TOK, 2 * TOK), G[p])

    def rs_copy(p, r, d, n, sub, places):
        return remote(
            SB.at[p, r, d, n, sub], RB.at[p, r, d, n, sub],
            rs_send.at[p], rs_recv.at[p, r, d, n, sub], neighbour(r, (1 - 2 * d) * places),
        )

    def rs_out(p, r, d, n, sub, places, value):
        SB[p, r, d, n, sub] = value.astype(BF16)
        rs_copy(p, r, d, n, sub, places).start()

    def rs_in(p, r, d, n, sub):
        wait_bytes(RB.at[p, r, d, n, sub], rs_recv.at[p, r, d, n, sub])
        return RB[p, r, d, n, sub].astype(F32)

    def rs_begin(p):
        for r in range(2):
            part = partial(p, r, 4)
            for d in range(2):
                rs_out(p, r, d, 0, d, 2, part[d * H:(d + 1) * H])
        for r in range(2):
            for d in range(2):
                part = partial(p, r, 3 * (1 - 2 * d))
                for sub in range(2):
                    rs_out(p, r, d, 1, sub, 1, part[sub * H:(sub + 1) * H])

    def rs_middle(p, n, places):
        for r in range(2):
            for d in range(2):
                part = partial(p, r, 2 * (1 - 2 * d))
                for sub in range(2):
                    value = part[sub * H:(sub + 1) * H] + rs_in(p, r, d, 1, sub)
                    if sub == d:
                        value += rs_in(p, r, d, 0, sub)
                    rs_out(p, r, d, n, sub, places, value)

    def rs_near(p, n, arrived=None):
        for r in range(2):
            for d in range(2):
                part = partial(p, r, 1 - 2 * d)
                for sub in range(2):
                    value = part[sub * H:(sub + 1) * H]
                    if arrived is not None:
                        value += rs_in(p, r, d, arrived, sub)
                    rs_out(p, r, d, n, sub, 1, value)

    def rs_own(p, arrivals):
        for r in range(2):
            own = partial(p, r, 0)
            for sub in range(2):
                total = own[sub * H:(sub + 1) * H]
                for d in range(2):
                    for n in arrivals:
                        total += rs_in(p, r, d, n, sub)
                YS[r, pl.ds(sub * 8, 8), p] = total.astype(BF16).reshape(8, 16, HD)

    def rs_direct(p):
        for kk in FAR:
            for r in range(2):
                for xh in range(2):
                    if r == 0:
                        src = YS.at[0, xh * 8 + (y + kk) % NY, p]
                        dst = XR.at[x * 8 + y, p]
                    else:
                        src = YS.at[1, (z + kk) % NZ * 2 + xh, p]
                        dst = XR.at[x * 8 + z, p]
                    cp = remote(src, dst, rs_d_send.at[p], rs_d_recv.at[p], owner(r, xh, kk))
                    if kk == 0:
                        is_me = (r == c) & (c * 2 + xh == x)

                        @pl.when(jnp.logical_not(is_me))
                        def _():
                            cp.start()

                        @pl.when(is_me)
                        def _():
                            pltpu.make_async_copy(src, dst, rs_d_recv.at[p]).start()
                    else:
                        cp.start()

    wait_bytes(G.at[V, theirs], g_sem.at[2 + V])
    rs_begin(V)

    kv_copy(V).wait_recv()
    vb = (kvs[V, mine] + kvr[V]).astype(BF16)
    gk = jnp.zeros((TOK, HD), F32)
    for h in range(0, GH, 2):
        pr = prob_s[h // 2]
        dp = dot(vb, pair(gov, h), NT)
        inner = jnp.sum(pr * dp, axis=0, keepdims=True)
        ds = (pr * (dp - inner) * SCALE).astype(BF16)
        gk += dot(ds, pair(qv, h))
    G[K, mine] = gk.astype(BF16)
    g_copy(K).start()

    def grad_tokens(zz):
        wz = jnp.concatenate([rows(K, zz), rows(V, zz)], axis=1)
        g = jnp.concatenate([G[K], G[V]], axis=1)
        GT[zz] = dot(g, wz, NT).astype(BF16)
        gtok[:, cols(zz, c)] = GT[zz, mine]
        remote(GT.at[zz, theirs], gtok.at[:, cols(zz, c)], gt_sem.at[0], gt_sem.at[1], at(x, y, z, other)).start()

    def attend_out(h):
        attn[:, h * HD:(h + 1) * HD] = dot(low_s[h // 2, :, h % 2 * TOK:(h % 2 + 1) * TOK], vb, TN).astype(BF16)

    for h in range(GH):
        attend_out(h)
    wait_bytes(G.at[K, theirs], g_sem.at[2 + K])
    rs_begin(K)
    rs_near(K, 2)
    rs_middle(V, 2, 1)
    for zz in range(4):
        grad_tokens(zz)
    rs_near(V, 3, 2)
    rs_middle(K, 3, 2)
    for zz in range(4, NZ):
        grad_tokens(zz)
    rs_own(V, (3,))
    rs_direct(V)
    rs_own(K, (2, 3))
    rs_direct(K)

    for k in range(2):
        wait_bytes(gtok.at[:, pl.ds(0, HALF)], gt_sem.at[k])
    for p in range(2):
        wait_bytes(W.at[p, pl.ds(0, 14)], ag_send.at[p])
        wait_bytes(W.at[p, pl.ds(0, 14)], rs_send.at[p])
        kv_copy(p).wait_send()
        g_copy(p).wait_send()
    wait_bytes(X.at[:, mine], tok_sem.at[0])

    @pl.when(home == c)
    def _():
        wait_bytes(XR.at[pl.ds(0, 31)], ag_d_send)

    @pl.when(home != c)
    def _():
        wait_bytes(XR, ag_d_send)

    for p in (V, K):
        wait_bytes(XR.at[:, p], rs_d_recv.at[p])
        gw[:, p * HD:(p + 1) * HD] = jnp.sum(XR[:, p].astype(F32), axis=0)

    @pl.when(home == c)
    def _():
        for p in range(2):
            wait_bytes(XR.at[pl.ds(0, 31), p], rs_d_send.at[p])

    @pl.when(home != c)
    def _():
        for p in range(2):
            wait_bytes(XR.at[:, p], rs_d_send.at[p])


OUTS = (((TOK, GH * HD), BF16), ((TOK, D), BF16), ((16, 2 * HD), F32))


def write_out(*refs):
    copies = [pltpu.make_async_copy(refs[i], refs[3 + i], refs[6].at[i]) for i in range(3)]
    for copy in copies:
        copy.start()
    for copy in copies:
        copy.wait()


def shards(tokens, queries, grad_out, seg_ids, w_values, w_scales):
    vmem = pl.BlockSpec(memory_space=pltpu.VMEM)
    hbm = pl.BlockSpec(memory_space=pltpu.HBM)
    dma = pltpu.SemaphoreType.DMA
    inner = pl.pallas_call(
        kernel,
        out_shape=tuple(pltpu.VMEM(shape, dtype) for shape, dtype in OUTS),
        in_specs=[hbm] * 6,
        out_specs=(vmem, vmem, vmem),
        scratch_shapes=[
            pltpu.VMEM((1, TOK), jnp.int32),
            pltpu.VMEM((16, 2 * HD), BF16),
            pltpu.VMEM((1, 4), BF16),
            pltpu.VMEM((NZ, 2 * TOK, BLK), BF16),
            pltpu.VMEM((2 * NZ, NY, 2, 16, 2 * TOK), BF16),
            pltpu.VMEM((2, 2 * NZ, NY, 2, 16, HD), BF16),
            pltpu.VMEM((NZ, 2 * TOK, BLK), BF16),
            pltpu.VMEM((TOK, GH * HD), BF16),
            pltpu.VMEM((TOK, GH * HD), BF16),
            pltpu.VMEM((GH // 2, TOK, 2 * TOK), F32),
            pltpu.VMEM((GH // 2, TOK, 2 * TOK), BF16),
            pltpu.VMEM((2, 16, HD), BF16),
            pltpu.VMEM((2, 2 * TOK, HD), F32),
            pltpu.VMEM((2, TOK, HD), F32),
            pltpu.VMEM((2, 2 * TOK, HD), BF16),
            pltpu.VMEM((2, 2, 2, 4, 2, TOK, HD), BF16),
            pltpu.VMEM((2, 2, 2, 4, 2, TOK, HD), BF16),
            pltpu.VMEM((2, 16, 2, 16, HD), BF16),
            pltpu.VMEM((32, 2, 16, HD), BF16),
            dma((6,)), dma((2,)), dma, dma((2,)), dma((2,)), dma((2, 2, 2, 4, 2)),
            dma((4,)), dma((4,)), dma((2,)), dma((2,)), dma((2, 2, 2, 4, 2)), dma((2,)), dma((2,)),
        ],
        compiler_params=pltpu.CompilerParams(
            collective_id=0, has_side_effects=True, vmem_limit_bytes=60 * 2**20
        ),
        cost_estimate=pl.CostEstimate(flops=2 * 10**9, bytes_accessed=5 * 2**20, transcendentals=131072),
        name="layer",
    )(tokens, queries, grad_out, seg_ids, w_values, w_scales.reshape(1, 4))
    return tuple(pl.pallas_call(
        write_out,
        out_shape=tuple(jax.ShapeDtypeStruct(shape, dtype) for shape, dtype in OUTS),
        in_specs=[vmem] * 3,
        out_specs=(pl.BlockSpec(memory_space=pl.ANY),) * 3,
        scratch_shapes=[dma((3,))],
        compiler_params=pltpu.CompilerParams(vmem_limit_bytes=4 * 2**20),
        name="write_out",
    )(*inner))


def solution(mesh):
    spec = P(("node", "dev"), None)
    return jax.shard_map(
        shards,
        mesh=mesh,
        in_specs=(spec, spec, spec, spec, spec, P()),
        out_specs=(spec, spec, spec),
        check_vma=False,
    )
```

```python
import jax
import jax.numpy as jnp
from jax import lax
from jax.experimental import pallas as pl
from jax.experimental.pallas import tpu as pltpu
from jax.sharding import PartitionSpec as P

HD = 128
GH = 8
NX, NY, NZ = 4, 8, 8
TOK = 128
D = 8192
HALF = D // 2
BLK = HALF // NZ
SCALE = HD ** (-0.5)
MESH = pl.DeviceIdType.MESH
F32, BF16 = jnp.float32, jnp.bfloat16
NT = (((1,), (1,)), ((), ()))
TN = (((0,), (0,)), ((), ()))
NN = (((1,), (0,)), ((), ()))
K, V = 0, 1
FAR_X = (2, 1, 3, 0)
FAR = (4, 3, 5, 2, 6, 1, 7, 0)


def dot(a, b, dims=NN):
    return lax.dot_general(a, b, dims, preferred_element_type=F32)


def wait_bytes(ref, sem):
    pltpu.make_async_copy(ref, ref, sem).wait()


def kernel(
    tok, q_hbm, go_hbm, seg_hbm, w_hbm, scales_hbm,
    attn, gtok, gw,
    seg, w, scales, X, XT, W, GT, qv, gov, prob_s, low_s, sh, kvs, kvr, G, SB, RB, YS, XR,
    l_sem, tok_sem, ag_d_send, ag_d_recv, ag_send, ag_recv,
    kv_sem, g_sem, gt_sem, rs_send, rs_recv, rs_d_send, rs_d_recv,
):
    node, dev = lax.axis_index("node"), lax.axis_index("dev")
    z, x = node // NX, node % NX
    y, c = dev // 2, dev % 2
    other = 1 - c
    home = x // 2

    def at(x, y, z, c):
        return {"node": z * NX + x, "dev": y * 2 + c}

    def remote(src, dst, ss, rs, target):
        return pltpu.make_async_remote_copy(
            src_ref=src, dst_ref=dst, send_sem=ss, recv_sem=rs, device_id=target, device_id_type=MESH
        )

    def cols(zz, core):
        return pl.ds(pl.multiple_of(zz * 2 * BLK + core * BLK, BLK), BLK)

    mine = pl.ds(pl.multiple_of(c * TOK, TOK), TOK)
    theirs = pl.ds(pl.multiple_of(other * TOK, TOK), TOK)

    bar = pltpu.get_barrier_semaphore()

    def greet(device):
        pl.semaphore_signal(bar, inc=1, device_id=device, device_id_type=MESH)

    def gather_target(kx, kk):
        return at((x + kx) % NX, (y + kk * other) % NY, (z + kk * c) % NZ, home)

    def owner(r, xh, kk):
        return at(c * 2 + xh, (y + kk) % NY if r == 0 else y, z if r == 0 else (z + kk) % NZ, r)

    for kk in FAR:
        for kx in FAR_X:
            if kk == 0 and kx == 0:
                @pl.when(home != c)
                def _():
                    greet(gather_target(0, 0))
            else:
                greet(gather_target(kx, kk))
        for r in range(2):
            for xh in range(2):
                if kk == 0:
                    @pl.when(jnp.logical_not((r == c) & (c * 2 + xh == x)))
                    def _():
                        greet(owner(r, xh, 0))
                else:
                    greet(owner(r, xh, kk))
    for step in (1, 2, 6, 7):
        greet(at(x, (y + step) % NY, z, c))
        greet(at(x, y, (z + step) % NZ, c))
    greet(at(x, y, z, other))

    small = [
        pltpu.make_async_copy(src, dst, l_sem.at[3 + n])
        for n, (src, dst) in enumerate(((w_hbm, w), (scales_hbm, scales), (seg_hbm, seg)))
    ]
    for copy in small:
        copy.start()
    for zz in range(NZ):
        pltpu.make_async_copy(tok.at[:, cols(zz, c)], X.at[zz, mine], l_sem.at[0]).start()
    q_copy = pltpu.make_async_copy(q_hbm, qv, l_sem.at[1])
    go_copy = pltpu.make_async_copy(go_hbm, gov, l_sem.at[2])
    q_copy.start()
    go_copy.start()

    small[0].wait()
    small[1].wait()
    pick = lax.broadcasted_iota(jnp.int32, (1, 4), 1) == z // 2
    scale = jnp.sum(jnp.where(pick, scales[...].astype(F32), 0.0), axis=1, keepdims=True)
    scaled = (w[...].astype(F32) * scale).astype(BF16)
    sh[K] = scaled[:, :HD]
    sh[V] = scaled[:, HD:]

    @pl.when(home == c)
    def _():
        pl.semaphore_wait(bar, 71)

    @pl.when(home != c)
    def _():
        pl.semaphore_wait(bar, 73)

    place = W.at[:, z * 2 + x % 2, y, c]
    for kk in FAR:
        for kx in FAR_X:
            cp = remote(sh, place, ag_d_send, ag_d_recv.at[c], gather_target(kx, kk))
            if kk == 0 and kx == 0:
                @pl.when(home != c)
                def _():
                    cp.start()

                @pl.when(home == c)
                def _():
                    pltpu.make_async_copy(sh, place, ag_d_recv.at[c]).start()
            else:
                cp.start()

    for zz in range(NZ):
        remote(tok.at[:, cols(zz, other)], X.at[zz, mine], tok_sem.at[0], tok_sem.at[1], at(x, y, z, other)).start()

    wait_bytes(X.at[:, mine], l_sem.at[0])
    wait_bytes(X.at[:, theirs], tok_sem.at[1])

    def turn(zz):
        XT[pl.ds(2 * zz, 2)] = X[zz].T.reshape(2, NY, 2, 16, 2 * TOK)

    for zz in range(4):
        turn(zz)

    def piece(p, r, i, sub):
        if r == 0:
            return W.at[p, i * 2 + sub, :, 0]
        return W.at[p, pl.ds(sub * NZ, NZ), i, 1]

    def neighbour(r, step):
        if r == 0:
            return at(x, y, (z + step + NZ) % NZ, c)
        return at(x, (y + step + NY) % NY, z, c)

    pos = (z, y)

    def ag_copy(p, r, d, k, places, sub):
        step = 1 - 2 * d
        part = piece(p, r, (pos[r] - step * k + 8) % 8, sub)
        return remote(part, part, ag_send.at[p], ag_recv.at[p, r, d, k + places - 1, sub], neighbour(r, step * places))

    def ag_arrival(p, r, d, k, sub):
        wait_bytes(piece(p, r, (pos[r] - (1 - 2 * d) * k + 8) % 8, sub), ag_recv.at[p, r, d, k - 1, sub])

    GOES = ({0: (1,), 1: (1,), 2: (2, 1)},) * 2

    def ag_pass(p, k):
        for sub in range(2):
            for r in range(2):
                for d in range(2):
                    if k == 4 and sub != d:
                        continue
                    if k > 0:
                        ag_arrival(p, r, d, k, sub)
                    for places in GOES[p].get(k, ()):
                        if k + places < 4 or sub == d:
                            ag_copy(p, r, d, k, places, sub).start()

    wait_bytes(W.at[:, pl.ds(z * 2, 2), :, 0], ag_d_recv.at[0])
    wait_bytes(W.at[:, :, y, 1], ag_d_recv.at[1])
    ag_pass(K, 0)
    ag_pass(V, 0)
    for zz in range(4, 6):
        turn(zz)
    ag_pass(K, 1)
    ag_pass(V, 1)
    for zz in range(6, 8):
        turn(zz)
    ag_pass(K, 2)
    ag_pass(V, 2)

    def kv_copy(p):
        return remote(kvs.at[p, theirs], kvr.at[p], kv_sem.at[p], kv_sem.at[2 + p], at(x, y, z, other))

    def rows(p, zz):
        return W[p, pl.ds(2 * zz, 2)].reshape(BLK, HD)

    def project(p):
        ag_pass(p, 3)
        ag_pass(p, 4)
        acc = jnp.zeros((2 * TOK, HD), F32)
        for zz in range(NZ):
            acc += dot(X[zz], rows(p, zz))
        kvs[p] = acc
        kv_copy(p).start()

    project(K)
    small[2].wait()
    seg_t = jnp.broadcast_to(seg[...].astype(F32), (TOK, TOK))
    seg_s = seg_t.T
    s_at = lax.broadcasted_iota(jnp.int32, (TOK, TOK), 0)
    t_at = lax.broadcasted_iota(jnp.int32, (TOK, TOK), 1)
    one = jnp.where((s_at <= t_at) & (seg_s == seg_t), 1.0, 0.0)
    allowed = jnp.concatenate([one, one], axis=1) > 0.5
    q_copy.wait()
    go_copy.wait()

    def pair(ref, h):
        return jnp.concatenate([ref[:, h * HD:(h + 1) * HD], ref[:, (h + 1) * HD:(h + 2) * HD]], axis=0)

    def g_copy(p):
        return remote(G.at[p, mine], G.at[p, mine], g_sem.at[p], g_sem.at[2 + p], at(x, y, z, other))

    kv_copy(K).wait_recv()
    kb = (kvs[K, mine] + kvr[K]).astype(BF16)
    gv = jnp.zeros((TOK, HD), F32)
    for h in range(0, GH, 2):
        st = jnp.where(allowed, dot(kb, pair(qv, h), NT) * SCALE, -1e30)
        top = jnp.max(st, axis=0, keepdims=True)
        ex = jnp.where(allowed, jnp.exp(st - top), 0.0)
        pr = ex * (1.0 / jnp.sum(ex, axis=0, keepdims=True))
        low = pr.astype(BF16)
        prob_s[h // 2] = pr
        low_s[h // 2] = low
        gv += dot(low, pair(gov, h))
    G[V, mine] = gv.astype(BF16)
    g_copy(V).start()

    project(V)

    H = TOK

    def partial(p, r, places):
        i = (pos[r] + places + 8) % 8
        if r == 0:
            lhs = XT[pl.ds(2 * i, 2), :, 0]
        else:
            lhs = XT[:, i, 1]
        return dot(lhs.reshape(2 * TOK, 2 * TOK), G[p])

    def rs_copy(p, r, d, n, sub, places):
        return remote(
            SB.at[p, r, d, n, sub], RB.at[p, r, d, n, sub],
            rs_send.at[p], rs_recv.at[p, r, d, n, sub], neighbour(r, (1 - 2 * d) * places),
        )

    def rs_out(p, r, d, n, sub, places, value):
        SB[p, r, d, n, sub] = value.astype(BF16)
        rs_copy(p, r, d, n, sub, places).start()

    def rs_in(p, r, d, n, sub):
        wait_bytes(RB.at[p, r, d, n, sub], rs_recv.at[p, r, d, n, sub])
        return RB[p, r, d, n, sub].astype(F32)

    def rs_begin(p):
        for r in range(2):
            part = partial(p, r, 4)
            for d in range(2):
                rs_out(p, r, d, 0, d, 2, part[d * H:(d + 1) * H])
        for r in range(2):
            for d in range(2):
                part = partial(p, r, 3 * (1 - 2 * d))
                for sub in range(2):
                    rs_out(p, r, d, 1, sub, 1, part[sub * H:(sub + 1) * H])

    def rs_middle(p, n, places):
        for r in range(2):
            for d in range(2):
                part = partial(p, r, 2 * (1 - 2 * d))
                for sub in range(2):
                    value = part[sub * H:(sub + 1) * H] + rs_in(p, r, d, 1, sub)
                    if sub == d:
                        value += rs_in(p, r, d, 0, sub)
                    rs_out(p, r, d, n, sub, places, value)

    def rs_near(p, n, arrived=None):
        for r in range(2):
            for d in range(2):
                part = partial(p, r, 1 - 2 * d)
                for sub in range(2):
                    value = part[sub * H:(sub + 1) * H]
                    if arrived is not None:
                        value += rs_in(p, r, d, arrived, sub)
                    rs_out(p, r, d, n, sub, 1, value)

    def rs_own(p, arrivals):
        for r in range(2):
            own = partial(p, r, 0)
            for sub in range(2):
                total = own[sub * H:(sub + 1) * H]
                for d in range(2):
                    for n in arrivals:
                        total += rs_in(p, r, d, n, sub)
                YS[r, pl.ds(sub * 8, 8), p] = total.astype(BF16).reshape(8, 16, HD)

    def rs_direct(p):
        for kk in FAR:
            for r in range(2):
                for xh in range(2):
                    if r == 0:
                        src = YS.at[0, xh * 8 + (y + kk) % NY, p]
                        dst = XR.at[x * 8 + y, p]
                    else:
                        src = YS.at[1, (z + kk) % NZ * 2 + xh, p]
                        dst = XR.at[x * 8 + z, p]
                    cp = remote(src, dst, rs_d_send.at[p], rs_d_recv.at[p], owner(r, xh, kk))
                    if kk == 0:
                        is_me = (r == c) & (c * 2 + xh == x)

                        @pl.when(jnp.logical_not(is_me))
                        def _():
                            cp.start()

                        @pl.when(is_me)
                        def _():
                            pltpu.make_async_copy(src, dst, rs_d_recv.at[p]).start()
                    else:
                        cp.start()

    wait_bytes(G.at[V, theirs], g_sem.at[2 + V])
    rs_begin(V)

    kv_copy(V).wait_recv()
    vb = (kvs[V, mine] + kvr[V]).astype(BF16)
    gk = jnp.zeros((TOK, HD), F32)
    for h in range(0, GH, 2):
        pr = prob_s[h // 2]
        dp = dot(vb, pair(gov, h), NT)
        inner = jnp.sum(pr * dp, axis=0, keepdims=True)
        ds = (pr * (dp - inner) * SCALE).astype(BF16)
        gk += dot(ds, pair(qv, h))
    G[K, mine] = gk.astype(BF16)
    g_copy(K).start()

    def grad_tokens(zz):
        wz = jnp.concatenate([rows(K, zz), rows(V, zz)], axis=1)
        g = jnp.concatenate([G[K], G[V]], axis=1)
        GT[zz] = dot(g, wz, NT).astype(BF16)
        gtok[:, cols(zz, c)] = GT[zz, mine]
        remote(GT.at[zz, theirs], gtok.at[:, cols(zz, c)], gt_sem.at[0], gt_sem.at[1], at(x, y, z, other)).start()

    def attend_out(h):
        attn[:, h * HD:(h + 1) * HD] = dot(low_s[h // 2, :, h % 2 * TOK:(h % 2 + 1) * TOK], vb, TN).astype(BF16)

    wait_bytes(G.at[K, theirs], g_sem.at[2 + K])
    rs_begin(K)
    rs_middle(V, 2, 1)
    for h in range(GH):
        attend_out(h)
    rs_middle(K, 2, 1)
    for zz in range(4):
        grad_tokens(zz)
    rs_near(V, 3, 2)
    rs_near(K, 3, 2)
    for zz in range(4, NZ):
        grad_tokens(zz)
    rs_own(V, (3,))
    rs_direct(V)
    rs_own(K, (3,))
    rs_direct(K)

    for k in range(2):
        wait_bytes(gtok.at[:, pl.ds(0, HALF)], gt_sem.at[k])
    for p in range(2):
        wait_bytes(W.at[p, pl.ds(0, 14)], ag_send.at[p])
        wait_bytes(W.at[p, pl.ds(0, 14)], rs_send.at[p])
        kv_copy(p).wait_send()
        g_copy(p).wait_send()
    wait_bytes(X.at[:, mine], tok_sem.at[0])

    @pl.when(home == c)
    def _():
        wait_bytes(XR.at[pl.ds(0, 31)], ag_d_send)

    @pl.when(home != c)
    def _():
        wait_bytes(XR, ag_d_send)

    for p in (V, K):
        wait_bytes(XR.at[:, p], rs_d_recv.at[p])
        gw[:, p * HD:(p + 1) * HD] = jnp.sum(XR[:, p].astype(F32), axis=0)

    @pl.when(home == c)
    def _():
        for p in range(2):
            wait_bytes(XR.at[pl.ds(0, 31), p], rs_d_send.at[p])

    @pl.when(home != c)
    def _():
        for p in range(2):
            wait_bytes(XR.at[:, p], rs_d_send.at[p])


OUTS = (((TOK, GH * HD), BF16), ((TOK, D), BF16), ((16, 2 * HD), F32))


def write_out(*refs):
    copies = [pltpu.make_async_copy(refs[i], refs[3 + i], refs[6].at[i]) for i in range(3)]
    for copy in copies:
        copy.start()
    for copy in copies:
        copy.wait()


def shards(tokens, queries, grad_out, seg_ids, w_values, w_scales):
    vmem = pl.BlockSpec(memory_space=pltpu.VMEM)
    hbm = pl.BlockSpec(memory_space=pltpu.HBM)
    dma = pltpu.SemaphoreType.DMA
    inner = pl.pallas_call(
        kernel,
        out_shape=tuple(pltpu.VMEM(shape, dtype) for shape, dtype in OUTS),
        in_specs=[hbm] * 6,
        out_specs=(vmem, vmem, vmem),
        scratch_shapes=[
            pltpu.VMEM((1, TOK), jnp.int32),
            pltpu.VMEM((16, 2 * HD), BF16),
            pltpu.VMEM((1, 4), BF16),
            pltpu.VMEM((NZ, 2 * TOK, BLK), BF16),
            pltpu.VMEM((2 * NZ, NY, 2, 16, 2 * TOK), BF16),
            pltpu.VMEM((2, 2 * NZ, NY, 2, 16, HD), BF16),
            pltpu.VMEM((NZ, 2 * TOK, BLK), BF16),
            pltpu.VMEM((TOK, GH * HD), BF16),
            pltpu.VMEM((TOK, GH * HD), BF16),
            pltpu.VMEM((GH // 2, TOK, 2 * TOK), F32),
            pltpu.VMEM((GH // 2, TOK, 2 * TOK), BF16),
            pltpu.VMEM((2, 16, HD), BF16),
            pltpu.VMEM((2, 2 * TOK, HD), F32),
            pltpu.VMEM((2, TOK, HD), F32),
            pltpu.VMEM((2, 2 * TOK, HD), BF16),
            pltpu.VMEM((2, 2, 2, 4, 2, TOK, HD), BF16),
            pltpu.VMEM((2, 2, 2, 4, 2, TOK, HD), BF16),
            pltpu.VMEM((2, 16, 2, 16, HD), BF16),
            pltpu.VMEM((32, 2, 16, HD), BF16),
            dma((6,)), dma((2,)), dma, dma((2,)), dma((2,)), dma((2, 2, 2, 4, 2)),
            dma((4,)), dma((4,)), dma((2,)), dma((2,)), dma((2, 2, 2, 4, 2)), dma((2,)), dma((2,)),
        ],
        compiler_params=pltpu.CompilerParams(
            collective_id=0, has_side_effects=True, vmem_limit_bytes=60 * 2**20
        ),
        cost_estimate=pl.CostEstimate(flops=2 * 10**9, bytes_accessed=5 * 2**20, transcendentals=131072),
        name="layer",
    )(tokens, queries, grad_out, seg_ids, w_values, w_scales.reshape(1, 4))
    return tuple(pl.pallas_call(
        write_out,
        out_shape=tuple(jax.ShapeDtypeStruct(shape, dtype) for shape, dtype in OUTS),
        in_specs=[vmem] * 3,
        out_specs=(pl.BlockSpec(memory_space=pl.ANY),) * 3,
        scratch_shapes=[dma((3,))],
        compiler_params=pltpu.CompilerParams(vmem_limit_bytes=4 * 2**20),
        name="write_out",
    )(*inner))


def solution(mesh):
    spec = P(("node", "dev"), None)
    return jax.shard_map(
        shards,
        mesh=mesh,
        in_specs=(spec, spec, spec, spec, spec, P()),
        out_specs=(spec, spec, spec),
        check_vma=False,
    )
```

```python
import jax
import jax.numpy as jnp
from jax import lax
from jax.experimental import pallas as pl
from jax.experimental.pallas import tpu as pltpu
from jax.sharding import PartitionSpec as P

HD = 128
GH = 8
NX, NY, NZ = 4, 8, 8
TOK = 128
D = 8192
HALF = D // 2
BLK = HALF // NZ
SCALE = HD ** (-0.5)
MESH = pl.DeviceIdType.MESH
F32, BF16 = jnp.float32, jnp.bfloat16
NT = (((1,), (1,)), ((), ()))
TN = (((0,), (0,)), ((), ()))
NN = (((1,), (0,)), ((), ()))
K, V = 0, 1
FAR_X = (2, 1, 3, 0)
FAR = (4, 3, 5, 2, 6, 1, 7, 0)


def dot(a, b, dims=NN):
    return lax.dot_general(a, b, dims, preferred_element_type=F32)


def wait_bytes(ref, sem):
    pltpu.make_async_copy(ref, ref, sem).wait()


def kernel(
    tok, q_hbm, go_hbm, seg_hbm, w_hbm, scales_hbm,
    attn, gtok, gw,
    seg, w, scales, X, XT, W, GT, qv, gov, prob_s, low_s, sh, kvs, kvr, G, PB, SB, RB, YS, XR,
    l_sem, tok_sem, ag_d_send, ag_d_recv, ag_send, ag_recv,
    kv_sem, g_sem, gt_sem, rs_send, rs_recv, rs_d_send, rs_d_recv,
):
    node, dev = lax.axis_index("node"), lax.axis_index("dev")
    z, x = node // NX, node % NX
    y, c = dev // 2, dev % 2
    other = 1 - c
    home = x // 2

    def at(x, y, z, c):
        return {"node": z * NX + x, "dev": y * 2 + c}

    def remote(src, dst, ss, rs, target):
        return pltpu.make_async_remote_copy(
            src_ref=src, dst_ref=dst, send_sem=ss, recv_sem=rs, device_id=target, device_id_type=MESH
        )

    def cols(zz, core):
        return pl.ds(pl.multiple_of(zz * 2 * BLK + core * BLK, BLK), BLK)

    mine = pl.ds(pl.multiple_of(c * TOK, TOK), TOK)
    theirs = pl.ds(pl.multiple_of(other * TOK, TOK), TOK)

    small = [
        pltpu.make_async_copy(src, dst, l_sem.at[3 + n])
        for n, (src, dst) in enumerate(((w_hbm, w), (scales_hbm, scales), (seg_hbm, seg)))
    ]
    for copy in small:
        copy.start()

    bar = pltpu.get_barrier_semaphore()

    def greet(device):
        pl.semaphore_signal(bar, inc=1, device_id=device, device_id_type=MESH)

    def gather_target(kx, kk):
        return at((x + kx) % NX, (y + kk * other) % NY, (z + kk * c) % NZ, home)

    def owner(r, xh, kk):
        return at(c * 2 + xh, (y + kk) % NY if r == 0 else y, z if r == 0 else (z + kk) % NZ, r)

    for kk in FAR:
        for kx in FAR_X:
            if kk == 0 and kx == 0:
                @pl.when(home != c)
                def _():
                    greet(gather_target(0, 0))
            else:
                greet(gather_target(kx, kk))
        for r in range(2):
            for xh in range(2):
                if kk == 0:
                    @pl.when(jnp.logical_not((r == c) & (c * 2 + xh == x)))
                    def _():
                        greet(owner(r, xh, 0))
                else:
                    greet(owner(r, xh, kk))
    for step in (1, 2, 6, 7):
        greet(at(x, (y + step) % NY, z, c))
        greet(at(x, y, (z + step) % NZ, c))
    greet(at(x, y, z, other))

    for zz in range(NZ):
        pltpu.make_async_copy(tok.at[:, cols(zz, c)], X.at[zz, mine], l_sem.at[0]).start()
    q_copy = pltpu.make_async_copy(q_hbm, qv, l_sem.at[1])
    go_copy = pltpu.make_async_copy(go_hbm, gov, l_sem.at[2])
    q_copy.start()
    go_copy.start()

    small[0].wait()
    small[1].wait()
    pick = lax.broadcasted_iota(jnp.int32, (1, 4), 1) == z // 2
    scale = jnp.sum(jnp.where(pick, scales[...].astype(F32), 0.0), axis=1, keepdims=True)
    scaled = (w[...].astype(F32) * scale).astype(BF16)
    sh[K] = scaled[:, :HD]
    sh[V] = scaled[:, HD:]

    @pl.when(home == c)
    def _():
        pl.semaphore_wait(bar, 71)

    @pl.when(home != c)
    def _():
        pl.semaphore_wait(bar, 73)

    place = W.at[:, z * 2 + x % 2, y, c]
    for kk in FAR:
        for kx in FAR_X:
            cp = remote(sh, place, ag_d_send, ag_d_recv.at[c], gather_target(kx, kk))
            if kk == 0 and kx == 0:
                @pl.when(home != c)
                def _():
                    cp.start()

                @pl.when(home == c)
                def _():
                    pltpu.make_async_copy(sh, place, ag_d_recv.at[c]).start()
            else:
                cp.start()

    for zz in range(NZ):
        remote(tok.at[:, cols(zz, other)], X.at[zz, mine], tok_sem.at[0], tok_sem.at[1], at(x, y, z, other)).start()

    wait_bytes(X.at[:, mine], l_sem.at[0])
    wait_bytes(X.at[:, theirs], tok_sem.at[1])

    def turn(zz):
        XT[pl.ds(2 * zz, 2)] = X[zz].T.reshape(2, NY, 2, 16, 2 * TOK)

    for zz in range(4):
        turn(zz)

    def piece(p, r, i, sub):
        if r == 0:
            return W.at[p, i * 2 + sub, :, 0]
        return W.at[p, pl.ds(sub * NZ, NZ), i, 1]

    def neighbour(r, step):
        if r == 0:
            return at(x, y, (z + step + NZ) % NZ, c)
        return at(x, (y + step + NY) % NY, z, c)

    pos = (z, y)

    def ag_copy(p, r, d, k, places, sub):
        step = 1 - 2 * d
        part = piece(p, r, (pos[r] - step * k + 8) % 8, sub)
        return remote(part, part, ag_send.at[p], ag_recv.at[p, r, d, k + places - 1, sub], neighbour(r, step * places))

    def ag_arrival(p, r, d, k, sub):
        wait_bytes(piece(p, r, (pos[r] - (1 - 2 * d) * k + 8) % 8, sub), ag_recv.at[p, r, d, k - 1, sub])

    GOES = ({0: (1,), 1: (1,), 2: (2, 1)},) * 2

    def ag_pass(p, k):
        for sub in range(2):
            for r in range(2):
                for d in range(2):
                    if k == 4 and sub != d:
                        continue
                    if k > 0:
                        ag_arrival(p, r, d, k, sub)
                    for places in GOES[p].get(k, ()):
                        if k + places < 4 or sub == d:
                            ag_copy(p, r, d, k, places, sub).start()

    wait_bytes(W.at[:, pl.ds(z * 2, 2), :, 0], ag_d_recv.at[0])
    wait_bytes(W.at[:, :, y, 1], ag_d_recv.at[1])
    ag_pass(K, 0)
    ag_pass(V, 0)
    for zz in range(4, 6):
        turn(zz)
    ag_pass(K, 1)
    ag_pass(V, 1)
    for zz in range(6, 8):
        turn(zz)
    ag_pass(K, 2)
    ag_pass(V, 2)

    def kv_copy(p):
        return remote(kvs.at[p, theirs], kvr.at[p], kv_sem.at[p], kv_sem.at[2 + p], at(x, y, z, other))

    def rows(p, zz):
        return W[p, pl.ds(2 * zz, 2)].reshape(BLK, HD)

    def project(p):
        ag_pass(p, 3)
        ag_pass(p, 4)
        acc = jnp.zeros((2 * TOK, HD), F32)
        for zz in range(NZ):
            acc += dot(X[zz], rows(p, zz))
        kvs[p] = acc
        kv_copy(p).start()

    project(K)
    small[2].wait()
    seg_t = jnp.broadcast_to(seg[...].astype(F32), (TOK, TOK))
    seg_s = seg_t.T
    s_at = lax.broadcasted_iota(jnp.int32, (TOK, TOK), 0)
    t_at = lax.broadcasted_iota(jnp.int32, (TOK, TOK), 1)
    one = jnp.where((s_at <= t_at) & (seg_s == seg_t), 1.0, 0.0)
    allowed = jnp.concatenate([one, one], axis=1) > 0.5
    q_copy.wait()
    go_copy.wait()

    def pair(ref, h):
        return jnp.concatenate([ref[:, h * HD:(h + 1) * HD], ref[:, (h + 1) * HD:(h + 2) * HD]], axis=0)

    def g_copy(p):
        return remote(G.at[p, mine], G.at[p, mine], g_sem.at[p], g_sem.at[2 + p], at(x, y, z, other))

    kv_copy(K).wait_recv()
    kb = (kvs[K, mine] + kvr[K]).astype(BF16)
    gv = jnp.zeros((TOK, HD), F32)
    for h in range(0, GH, 2):
        st = jnp.where(allowed, dot(kb, pair(qv, h), NT) * SCALE, -1e30)
        top = jnp.max(st, axis=0, keepdims=True)
        ex = jnp.exp(st - top)
        pr = ex * (1.0 / jnp.sum(ex, axis=0, keepdims=True))
        low = pr.astype(BF16)
        prob_s[h // 2] = pr
        low_s[h // 2] = low
        gv += dot(low, pair(gov, h))
    G[V, mine] = gv.astype(BF16)
    g_copy(V).start()

    project(V)

    H = TOK

    def partial(p, r, places):
        i = (pos[r] + places + 8) % 8
        if r == 0:
            lhs = XT[pl.ds(2 * i, 2), :, 0]
        else:
            lhs = XT[:, i, 1]
        return dot(lhs.reshape(2 * TOK, 2 * TOK), G[p])

    def rs_copy(p, r, d, n, sub, places):
        return remote(
            SB.at[p, r, d, n, sub], RB.at[p, r, d, n, sub],
            rs_send.at[p], rs_recv.at[p, r, d, n, sub], neighbour(r, (1 - 2 * d) * places),
        )

    def rs_out(p, r, d, n, sub, places, value):
        SB[p, r, d, n, sub] = value.astype(BF16)
        rs_copy(p, r, d, n, sub, places).start()

    def rs_in(p, r, d, n, sub):
        wait_bytes(RB.at[p, r, d, n, sub], rs_recv.at[p, r, d, n, sub])
        return RB[p, r, d, n, sub].astype(F32)

    def rs_begin(p):
        for r in range(2):
            part = partial(p, r, 4)
            for d in range(2):
                rs_out(p, r, d, 0, d, 2, part[d * H:(d + 1) * H])
        for r in range(2):
            for d in range(2):
                part = partial(p, r, 3 * (1 - 2 * d))
                for sub in range(2):
                    rs_out(p, r, d, 1, sub, 1, part[sub * H:(sub + 1) * H])

    def rs_ahead(p):
        for r in range(2):
            for n, places in enumerate((2, -2, 1, -1, 0)):
                PB[p, r, n] = partial(p, r, places)

    def rs_middle(p):
        for sub in range(2):
            for r in range(2):
                for d in range(2):
                    value = PB[p, r, d, sub * H:(sub + 1) * H] + rs_in(p, r, d, 1, sub)
                    if sub == d:
                        value += rs_in(p, r, d, 0, sub)
                    rs_out(p, r, d, 2, sub, 1, value)

    def rs_near(p):
        for sub in range(2):
            for r in range(2):
                for d in range(2):
                    rs_out(p, r, d, 3, sub, 1, PB[p, r, 2 + d, sub * H:(sub + 1) * H] + rs_in(p, r, d, 2, sub))

    def rs_own(p, r):
        for sub in range(2):
            total = PB[p, r, 4, sub * H:(sub + 1) * H]
            for d in range(2):
                total += rs_in(p, r, d, 3, sub)
            YS[r, pl.ds(sub * 8, 8), p] = total.astype(BF16).reshape(8, 16, HD)

    def rs_direct(p, r):
        for kk in FAR:
            for xh in range(2):
                if r == 0:
                    src = YS.at[0, xh * 8 + (y + kk) % NY, p]
                    dst = XR.at[x * 8 + y, p]
                else:
                    src = YS.at[1, (z + kk) % NZ * 2 + xh, p]
                    dst = XR.at[x * 8 + z, p]
                cp = remote(src, dst, rs_d_send.at[p], rs_d_recv.at[p], owner(r, xh, kk))
                if kk == 0:
                    is_me = (r == c) & (c * 2 + xh == x)

                    @pl.when(jnp.logical_not(is_me))
                    def _():
                        cp.start()

                    @pl.when(is_me)
                    def _():
                        pltpu.make_async_copy(src, dst, rs_d_recv.at[p]).start()
                else:
                    cp.start()

    wait_bytes(G.at[V, theirs], g_sem.at[2 + V])
    rs_begin(V)

    kv_copy(V).wait_recv()
    vb = (kvs[V, mine] + kvr[V]).astype(BF16)
    gk = jnp.zeros((TOK, HD), F32)
    for h in range(0, GH, 2):
        pr = prob_s[h // 2]
        dp = dot(vb, pair(gov, h), NT)
        inner = jnp.sum(pr * dp, axis=0, keepdims=True)
        ds = (pr * (dp - inner) * SCALE).astype(BF16)
        gk += dot(ds, pair(qv, h))
    G[K, mine] = gk.astype(BF16)
    g_copy(K).start()

    def grad_tokens(zz):
        wz = jnp.concatenate([rows(K, zz), rows(V, zz)], axis=1)
        g = jnp.concatenate([G[K], G[V]], axis=1)
        GT[zz] = dot(g, wz, NT).astype(BF16)
        gtok[:, cols(zz, c)] = GT[zz, mine]
        remote(GT.at[zz, theirs], gtok.at[:, cols(zz, c)], gt_sem.at[0], gt_sem.at[1], at(x, y, z, other)).start()

    def attend_out(h):
        attn[:, h * HD:(h + 1) * HD] = dot(low_s[h // 2, :, h % 2 * TOK:(h % 2 + 1) * TOK], vb, TN).astype(BF16)

    rs_ahead(V)
    wait_bytes(G.at[K, theirs], g_sem.at[2 + K])
    rs_begin(K)
    rs_middle(V)
    rs_ahead(K)
    rs_middle(K)
    rs_near(V)
    for zz in range(0, 4):
        grad_tokens(zz)
    rs_near(K)
    for zz in range(4, 8):
        grad_tokens(zz)
    for r in range(2):
        rs_own(V, r)
        rs_direct(V, r)
    for r in range(2):
        rs_own(K, r)
        rs_direct(K, r)
    for h in range(GH):
        attend_out(h)

    for k in range(2):
        wait_bytes(gtok.at[:, pl.ds(0, HALF)], gt_sem.at[k])
    for p in range(2):
        wait_bytes(W.at[p, pl.ds(0, 14)], ag_send.at[p])
        wait_bytes(W.at[p, pl.ds(0, 14)], rs_send.at[p])
        kv_copy(p).wait_send()
        g_copy(p).wait_send()
    wait_bytes(X.at[:, mine], tok_sem.at[0])

    @pl.when(home == c)
    def _():
        wait_bytes(XR.at[pl.ds(0, 31)], ag_d_send)

    @pl.when(home != c)
    def _():
        wait_bytes(XR, ag_d_send)

    for p in (V, K):
        wait_bytes(XR.at[:, p], rs_d_recv.at[p])
        gw[:, p * HD:(p + 1) * HD] = jnp.sum(XR[:, p].astype(F32), axis=0)

    @pl.when(home == c)
    def _():
        for p in range(2):
            wait_bytes(XR.at[pl.ds(0, 31), p], rs_d_send.at[p])

    @pl.when(home != c)
    def _():
        for p in range(2):
            wait_bytes(XR.at[:, p], rs_d_send.at[p])


OUTS = (((TOK, GH * HD), BF16), ((TOK, D), BF16), ((16, 2 * HD), F32))


def write_out(*refs):
    copies = [pltpu.make_async_copy(refs[i], refs[3 + i], refs[6].at[i]) for i in range(3)]
    for copy in copies:
        copy.start()
    for copy in copies:
        copy.wait()


def shards(tokens, queries, grad_out, seg_ids, w_values, w_scales):
    vmem = pl.BlockSpec(memory_space=pltpu.VMEM)
    hbm = pl.BlockSpec(memory_space=pltpu.HBM)
    dma = pltpu.SemaphoreType.DMA
    inner = pl.pallas_call(
        kernel,
        out_shape=tuple(pltpu.VMEM(shape, dtype) for shape, dtype in OUTS),
        in_specs=[hbm] * 6,
        out_specs=(vmem, vmem, vmem),
        scratch_shapes=[
            pltpu.VMEM((1, TOK), jnp.int32),
            pltpu.VMEM((16, 2 * HD), BF16),
            pltpu.VMEM((1, 4), BF16),
            pltpu.VMEM((NZ, 2 * TOK, BLK), BF16),
            pltpu.VMEM((2 * NZ, NY, 2, 16, 2 * TOK), BF16),
            pltpu.VMEM((2, 2 * NZ, NY, 2, 16, HD), BF16),
            pltpu.VMEM((NZ, 2 * TOK, BLK), BF16),
            pltpu.VMEM((TOK, GH * HD), BF16),
            pltpu.VMEM((TOK, GH * HD), BF16),
            pltpu.VMEM((GH // 2, TOK, 2 * TOK), F32),
            pltpu.VMEM((GH // 2, TOK, 2 * TOK), BF16),
            pltpu.VMEM((2, 16, HD), BF16),
            pltpu.VMEM((2, 2 * TOK, HD), F32),
            pltpu.VMEM((2, TOK, HD), F32),
            pltpu.VMEM((2, 2 * TOK, HD), BF16),
            pltpu.VMEM((2, 2, 5, 2 * TOK, HD), F32),
            pltpu.VMEM((2, 2, 2, 4, 2, TOK, HD), BF16),
            pltpu.VMEM((2, 2, 2, 4, 2, TOK, HD), BF16),
            pltpu.VMEM((2, 16, 2, 16, HD), BF16),
            pltpu.VMEM((32, 2, 16, HD), BF16),
            dma((6,)), dma((2,)), dma, dma((2,)), dma((2,)), dma((2, 2, 2, 4, 2)),
            dma((4,)), dma((4,)), dma((2,)), dma((2,)), dma((2, 2, 2, 4, 2)), dma((2,)), dma((2,)),
        ],
        compiler_params=pltpu.CompilerParams(
            collective_id=0, has_side_effects=True, vmem_limit_bytes=60 * 2**20
        ),
        cost_estimate=pl.CostEstimate(flops=2 * 10**9, bytes_accessed=5 * 2**20, transcendentals=131072),
        name="layer",
    )(tokens, queries, grad_out, seg_ids, w_values, w_scales.reshape(1, 4))
    return tuple(pl.pallas_call(
        write_out,
        out_shape=tuple(jax.ShapeDtypeStruct(shape, dtype) for shape, dtype in OUTS),
        in_specs=[vmem] * 3,
        out_specs=(pl.BlockSpec(memory_space=pl.ANY),) * 3,
        scratch_shapes=[dma((3,))],
        compiler_params=pltpu.CompilerParams(vmem_limit_bytes=4 * 2**20),
        name="write_out",
    )(*inner))


def solution(mesh):
    spec = P(("node", "dev"), None)
    return jax.shard_map(
        shards,
        mesh=mesh,
        in_specs=(spec, spec, spec, spec, spec, P()),
        out_specs=(spec, spec, spec),
        check_vma=False,
    )
```

```python
import jax
import jax.numpy as jnp
from jax import lax
from jax.experimental import pallas as pl
from jax.experimental.pallas import tpu as pltpu
from jax.sharding import PartitionSpec as P

HD = 128
GH = 8
NX, NY, NZ = 4, 8, 8
TOK = 128
D = 8192
HALF = D // 2
BLK = HALF // NZ
SCALE = HD ** (-0.5)
MESH = pl.DeviceIdType.MESH
F32, BF16 = jnp.float32, jnp.bfloat16
NT = (((1,), (1,)), ((), ()))
TN = (((0,), (0,)), ((), ()))
NN = (((1,), (0,)), ((), ()))
K, V = 0, 1
FAR_X = (2, 1, 3, 0)
FAR = (4, 3, 5, 2, 6, 1, 7, 0)


def dot(a, b, dims=NN):
    return lax.dot_general(a, b, dims, preferred_element_type=F32)


def wait_bytes(ref, sem):
    pltpu.make_async_copy(ref, ref, sem).wait()


def kernel(
    tok, q_hbm, go_hbm, seg_hbm, w_hbm, scales_hbm,
    attn, gtok, gw,
    seg, w, scales, X, XT, W, GT, qv, gov, prob_s, low_s, sh, kvs, kvr, G, PB, SB, RB, YS, XR,
    l_sem, tok_sem, ag_d_send, ag_d_recv, ag_send, ag_recv,
    kv_sem, g_sem, gt_sem, rs_send, rs_recv, rs_d_send, rs_d_recv,
):
    node, dev = lax.axis_index("node"), lax.axis_index("dev")
    z, x = node // NX, node % NX
    y, c = dev // 2, dev % 2
    other = 1 - c
    home = x // 2

    def at(x, y, z, c):
        return {"node": z * NX + x, "dev": y * 2 + c}

    def remote(src, dst, ss, rs, target):
        return pltpu.make_async_remote_copy(
            src_ref=src, dst_ref=dst, send_sem=ss, recv_sem=rs, device_id=target, device_id_type=MESH
        )

    def cols(zz, core):
        return pl.ds(pl.multiple_of(zz * 2 * BLK + core * BLK, BLK), BLK)

    mine = pl.ds(pl.multiple_of(c * TOK, TOK), TOK)
    theirs = pl.ds(pl.multiple_of(other * TOK, TOK), TOK)

    small = [
        pltpu.make_async_copy(src, dst, l_sem.at[3 + n])
        for n, (src, dst) in enumerate(((w_hbm, w), (scales_hbm, scales), (seg_hbm, seg)))
    ]
    for copy in small:
        copy.start()

    bar = pltpu.get_barrier_semaphore()

    def greet(device):
        pl.semaphore_signal(bar, inc=1, device_id=device, device_id_type=MESH)

    def gather_target(kx, kk):
        return at((x + kx) % NX, (y + kk * other) % NY, (z + kk * c) % NZ, home)

    def owner(r, xh, kk):
        return at(c * 2 + xh, (y + kk) % NY if r == 0 else y, z if r == 0 else (z + kk) % NZ, r)

    for kk in FAR:
        for kx in FAR_X:
            if kk == 0 and kx == 0:
                @pl.when(home != c)
                def _():
                    greet(gather_target(0, 0))
            else:
                greet(gather_target(kx, kk))
        for r in range(2):
            for xh in range(2):
                if kk == 0:
                    @pl.when(jnp.logical_not((r == c) & (c * 2 + xh == x)))
                    def _():
                        greet(owner(r, xh, 0))
                else:
                    greet(owner(r, xh, kk))
    for step in (1, 2, 6, 7):
        greet(at(x, (y + step) % NY, z, c))
        greet(at(x, y, (z + step) % NZ, c))
    greet(at(x, y, z, other))

    for zz in range(NZ):
        pltpu.make_async_copy(tok.at[:, cols(zz, c)], X.at[zz, mine], l_sem.at[0]).start()
    q_copy = pltpu.make_async_copy(q_hbm, qv, l_sem.at[1])
    go_copy = pltpu.make_async_copy(go_hbm, gov, l_sem.at[2])
    q_copy.start()
    go_copy.start()

    small[0].wait()
    small[1].wait()
    pick = lax.broadcasted_iota(jnp.int32, (1, 4), 1) == z // 2
    scale = jnp.sum(jnp.where(pick, scales[...].astype(F32), 0.0), axis=1, keepdims=True)
    scaled = (w[...].astype(F32) * scale).astype(BF16)
    sh[K] = scaled[:, :HD]
    sh[V] = scaled[:, HD:]

    @pl.when(home == c)
    def _():
        pl.semaphore_wait(bar, 71)

    @pl.when(home != c)
    def _():
        pl.semaphore_wait(bar, 73)

    place = W.at[:, z * 2 + x % 2, y, c]
    for kk in FAR:
        for kx in FAR_X:
            cp = remote(sh, place, ag_d_send, ag_d_recv.at[c], gather_target(kx, kk))
            if kk == 0 and kx == 0:
                @pl.when(home != c)
                def _():
                    cp.start()

                @pl.when(home == c)
                def _():
                    pltpu.make_async_copy(sh, place, ag_d_recv.at[c]).start()
            else:
                cp.start()

    for zz in range(NZ):
        remote(tok.at[:, cols(zz, other)], X.at[zz, mine], tok_sem.at[0], tok_sem.at[1], at(x, y, z, other)).start()

    wait_bytes(X.at[:, mine], l_sem.at[0])
    wait_bytes(X.at[:, theirs], tok_sem.at[1])

    def turn(zz):
        XT[pl.ds(2 * zz, 2)] = X[zz].T.reshape(2, NY, 2, 16, 2 * TOK)

    for zz in range(4):
        turn(zz)

    def piece(p, r, i, sub):
        if r == 0:
            return W.at[p, i * 2 + sub, :, 0]
        return W.at[p, pl.ds(sub * NZ, NZ), i, 1]

    def neighbour(r, step):
        if r == 0:
            return at(x, y, (z + step + NZ) % NZ, c)
        return at(x, (y + step + NY) % NY, z, c)

    pos = (z, y)

    def ag_copy(p, r, d, k, places, sub):
        step = 1 - 2 * d
        part = piece(p, r, (pos[r] - step * k + 8) % 8, sub)
        return remote(part, part, ag_send.at[p], ag_recv.at[p, r, d, k + places - 1, sub], neighbour(r, step * places))

    def ag_arrival(p, r, d, k, sub):
        wait_bytes(piece(p, r, (pos[r] - (1 - 2 * d) * k + 8) % 8, sub), ag_recv.at[p, r, d, k - 1, sub])

    GOES = ({0: (1,), 1: (1,), 2: (2, 1)},) * 2

    def ag_pass(p, k):
        for sub in range(2):
            for r in range(2):
                for d in range(2):
                    if k == 4 and sub != d:
                        continue
                    if k > 0:
                        ag_arrival(p, r, d, k, sub)
                    for places in GOES[p].get(k, ()):
                        if k + places < 4 or sub == d:
                            ag_copy(p, r, d, k, places, sub).start()

    wait_bytes(W.at[:, pl.ds(z * 2, 2), :, 0], ag_d_recv.at[0])
    wait_bytes(W.at[:, :, y, 1], ag_d_recv.at[1])
    ag_pass(K, 0)
    ag_pass(V, 0)
    for zz in range(4, 6):
        turn(zz)
    ag_pass(K, 1)
    ag_pass(V, 1)
    for zz in range(6, 8):
        turn(zz)
    ag_pass(K, 2)
    ag_pass(V, 2)

    def kv_copy(p):
        return remote(kvs.at[p, theirs], kvr.at[p], kv_sem.at[p], kv_sem.at[2 + p], at(x, y, z, other))

    def rows(p, zz):
        return W[p, pl.ds(2 * zz, 2)].reshape(BLK, HD)

    def project(p):
        ag_pass(p, 3)
        ag_pass(p, 4)
        for part in (theirs, mine):
            acc = jnp.zeros((TOK, HD), F32)
            for zz in range(NZ):
                acc += dot(X[zz, part], rows(p, zz))
            kvs[p, part] = acc
            if part is theirs:
                kv_copy(p).start()

    project(K)
    small[2].wait()
    seg_t = jnp.broadcast_to(seg[...].astype(F32), (TOK, TOK))
    seg_s = seg_t.T
    s_at = lax.broadcasted_iota(jnp.int32, (TOK, TOK), 0)
    t_at = lax.broadcasted_iota(jnp.int32, (TOK, TOK), 1)
    one = jnp.where((s_at <= t_at) & (seg_s == seg_t), 1.0, 0.0)
    allowed = jnp.concatenate([one] * GH, axis=1) > 0.5
    q_copy.wait()
    go_copy.wait()

    def stacked(ref):
        return jnp.concatenate([ref[:, h * HD:(h + 1) * HD] for h in range(GH)], axis=0)

    def g_copy(p):
        return remote(G.at[p, mine], G.at[p, mine], g_sem.at[p], g_sem.at[2 + p], at(x, y, z, other))

    kv_copy(K).wait_recv()
    kb = (kvs[K, mine] + kvr[K]).astype(BF16)
    st = jnp.where(allowed, dot(kb, stacked(qv), NT) * SCALE, -1e30)
    ex = jnp.exp(st - jnp.max(st, axis=0, keepdims=True))
    pr = ex * (1.0 / jnp.sum(ex, axis=0, keepdims=True))
    low = pr.astype(BF16)
    prob_s[...] = pr
    low_s[...] = low
    gv = dot(low, stacked(gov))
    G[V, mine] = gv.astype(BF16)
    g_copy(V).start()

    project(V)

    H = TOK

    def partial(p, r, places):
        i = (pos[r] + places + 8) % 8
        if r == 0:
            lhs = XT[pl.ds(2 * i, 2), :, 0]
        else:
            lhs = XT[:, i, 1]
        return dot(lhs.reshape(2 * TOK, 2 * TOK), G[p])

    def rs_copy(p, r, d, n, sub, places):
        return remote(
            SB.at[p, r, d, n, sub], RB.at[p, r, d, n, sub],
            rs_send.at[p], rs_recv.at[p, r, d, n, sub], neighbour(r, (1 - 2 * d) * places),
        )

    def rs_out(p, r, d, n, sub, places, value):
        SB[p, r, d, n, sub] = value.astype(BF16)
        rs_copy(p, r, d, n, sub, places).start()

    def rs_in(p, r, d, n, sub):
        wait_bytes(RB.at[p, r, d, n, sub], rs_recv.at[p, r, d, n, sub])
        return RB[p, r, d, n, sub].astype(F32)

    def rs_begin(p):
        for r in range(2):
            part = partial(p, r, 4)
            for d in range(2):
                rs_out(p, r, d, 0, d, 2, part[d * H:(d + 1) * H])
        for r in range(2):
            for d in range(2):
                part = partial(p, r, 3 * (1 - 2 * d))
                for sub in range(2):
                    rs_out(p, r, d, 1, sub, 1, part[sub * H:(sub + 1) * H])

    def rs_ahead(p):
        for r in range(2):
            for n, places in enumerate((2, -2, 1, -1, 0)):
                PB[p, r, n] = partial(p, r, places)

    def rs_middle(p):
        for sub in range(2):
            for r in range(2):
                for d in range(2):
                    value = PB[p, r, d, sub * H:(sub + 1) * H] + rs_in(p, r, d, 1, sub)
                    if sub == d:
                        value += rs_in(p, r, d, 0, sub)
                    rs_out(p, r, d, 2, sub, 1, value)

    def rs_near(p):
        for sub in range(2):
            for r in range(2):
                for d in range(2):
                    rs_out(p, r, d, 3, sub, 1, PB[p, r, 2 + d, sub * H:(sub + 1) * H] + rs_in(p, r, d, 2, sub))

    def rs_own(p, r):
        for sub in range(2):
            total = PB[p, r, 4, sub * H:(sub + 1) * H]
            for d in range(2):
                total += rs_in(p, r, d, 3, sub)
            YS[r, pl.ds(sub * 8, 8), p] = total.astype(BF16).reshape(8, 16, HD)

    def rs_direct(p, r):
        for kk in FAR:
            for xh in range(2):
                if r == 0:
                    src = YS.at[0, xh * 8 + (y + kk) % NY, p]
                    dst = XR.at[x * 8 + y, p]
                else:
                    src = YS.at[1, (z + kk) % NZ * 2 + xh, p]
                    dst = XR.at[x * 8 + z, p]
                cp = remote(src, dst, rs_d_send.at[p], rs_d_recv.at[p], owner(r, xh, kk))
                if kk == 0:
                    is_me = (r == c) & (c * 2 + xh == x)

                    @pl.when(jnp.logical_not(is_me))
                    def _():
                        cp.start()

                    @pl.when(is_me)
                    def _():
                        pltpu.make_async_copy(src, dst, rs_d_recv.at[p]).start()
                else:
                    cp.start()

    wait_bytes(G.at[V, theirs], g_sem.at[2 + V])
    rs_begin(V)

    kv_copy(V).wait_recv()
    vb = (kvs[V, mine] + kvr[V]).astype(BF16)
    pr = prob_s[...]
    dp = dot(vb, stacked(gov), NT)
    inner = jnp.sum(pr * dp, axis=0, keepdims=True)
    gk = dot((pr * (dp - inner) * SCALE).astype(BF16), stacked(qv))
    G[K, mine] = gk.astype(BF16)
    g_copy(K).start()

    def grad_tokens(zz):
        wz = jnp.concatenate([rows(K, zz), rows(V, zz)], axis=1)
        g = jnp.concatenate([G[K], G[V]], axis=1)
        GT[zz] = dot(g, wz, NT).astype(BF16)
        gtok[:, cols(zz, c)] = GT[zz, mine]
        remote(GT.at[zz, theirs], gtok.at[:, cols(zz, c)], gt_sem.at[0], gt_sem.at[1], at(x, y, z, other)).start()

    def attend_out(h):
        attn[:, h * HD:(h + 1) * HD] = dot(low_s[:, h * TOK:(h + 1) * TOK], vb, TN).astype(BF16)

    rs_ahead(V)
    wait_bytes(G.at[K, theirs], g_sem.at[2 + K])
    rs_begin(K)
    rs_middle(V)
    rs_ahead(K)
    rs_middle(K)
    rs_near(V)
    for zz in range(0, 4):
        grad_tokens(zz)
    rs_near(K)
    for zz in range(4, 8):
        grad_tokens(zz)
    for r in range(2):
        rs_own(V, r)
        rs_direct(V, r)
    for r in range(2):
        rs_own(K, r)
        rs_direct(K, r)
    for h in range(GH):
        attend_out(h)

    for k in range(2):
        wait_bytes(gtok.at[:, pl.ds(0, HALF)], gt_sem.at[k])
    for p in range(2):
        wait_bytes(W.at[p, pl.ds(0, 14)], ag_send.at[p])
        wait_bytes(W.at[p, pl.ds(0, 14)], rs_send.at[p])
        kv_copy(p).wait_send()
        g_copy(p).wait_send()
    wait_bytes(X.at[:, mine], tok_sem.at[0])

    @pl.when(home == c)
    def _():
        wait_bytes(XR.at[pl.ds(0, 31)], ag_d_send)

    @pl.when(home != c)
    def _():
        wait_bytes(XR, ag_d_send)

    for p in (V, K):
        wait_bytes(XR.at[:, p], rs_d_recv.at[p])
        gw[:, p * HD:(p + 1) * HD] = jnp.sum(XR[:, p].astype(F32), axis=0)

    @pl.when(home == c)
    def _():
        for p in range(2):
            wait_bytes(XR.at[pl.ds(0, 31), p], rs_d_send.at[p])

    @pl.when(home != c)
    def _():
        for p in range(2):
            wait_bytes(XR.at[:, p], rs_d_send.at[p])


OUTS = (((TOK, GH * HD), BF16), ((TOK, D), BF16), ((16, 2 * HD), F32))


def write_out(*refs):
    copies = [pltpu.make_async_copy(refs[i], refs[3 + i], refs[6].at[i]) for i in range(3)]
    for copy in copies:
        copy.start()
    for copy in copies:
        copy.wait()


def shards(tokens, queries, grad_out, seg_ids, w_values, w_scales):
    vmem = pl.BlockSpec(memory_space=pltpu.VMEM)
    hbm = pl.BlockSpec(memory_space=pltpu.HBM)
    dma = pltpu.SemaphoreType.DMA
    inner = pl.pallas_call(
        kernel,
        out_shape=tuple(pltpu.VMEM(shape, dtype) for shape, dtype in OUTS),
        in_specs=[hbm] * 6,
        out_specs=(vmem, vmem, vmem),
        scratch_shapes=[
            pltpu.VMEM((1, TOK), jnp.int32),
            pltpu.VMEM((16, 2 * HD), BF16),
            pltpu.VMEM((1, 4), BF16),
            pltpu.VMEM((NZ, 2 * TOK, BLK), BF16),
            pltpu.VMEM((2 * NZ, NY, 2, 16, 2 * TOK), BF16),
            pltpu.VMEM((2, 2 * NZ, NY, 2, 16, HD), BF16),
            pltpu.VMEM((NZ, 2 * TOK, BLK), BF16),
            pltpu.VMEM((TOK, GH * HD), BF16),
            pltpu.VMEM((TOK, GH * HD), BF16),
            pltpu.VMEM((TOK, GH * TOK), F32),
            pltpu.VMEM((TOK, GH * TOK), BF16),
            pltpu.VMEM((2, 16, HD), BF16),
            pltpu.VMEM((2, 2 * TOK, HD), F32),
            pltpu.VMEM((2, TOK, HD), F32),
            pltpu.VMEM((2, 2 * TOK, HD), BF16),
            pltpu.VMEM((2, 2, 5, 2 * TOK, HD), F32),
            pltpu.VMEM((2, 2, 2, 4, 2, TOK, HD), BF16),
            pltpu.VMEM((2, 2, 2, 4, 2, TOK, HD), BF16),
            pltpu.VMEM((2, 16, 2, 16, HD), BF16),
            pltpu.VMEM((32, 2, 16, HD), BF16),
            dma((6,)), dma((2,)), dma, dma((2,)), dma((2,)), dma((2, 2, 2, 4, 2)),
            dma((4,)), dma((4,)), dma((2,)), dma((2,)), dma((2, 2, 2, 4, 2)), dma((2,)), dma((2,)),
        ],
        compiler_params=pltpu.CompilerParams(
            collective_id=0, has_side_effects=True, vmem_limit_bytes=60 * 2**20
        ),
        cost_estimate=pl.CostEstimate(flops=2 * 10**9, bytes_accessed=5 * 2**20, transcendentals=131072),
        name="layer",
    )(tokens, queries, grad_out, seg_ids, w_values, w_scales.reshape(1, 4))
    return tuple(pl.pallas_call(
        write_out,
        out_shape=tuple(jax.ShapeDtypeStruct(shape, dtype) for shape, dtype in OUTS),
        in_specs=[vmem] * 3,
        out_specs=(pl.BlockSpec(memory_space=pl.ANY),) * 3,
        scratch_shapes=[dma((3,))],
        compiler_params=pltpu.CompilerParams(vmem_limit_bytes=4 * 2**20),
        name="write_out",
    )(*inner))


def solution(mesh):
    spec = P(("node", "dev"), None)
    return jax.shard_map(
        shards,
        mesh=mesh,
        in_specs=(spec, spec, spec, spec, spec, P()),
        out_specs=(spec, spec, spec),
        check_vma=False,
    )
```

```python
import jax
import jax.numpy as jnp
from jax import lax
from jax.experimental import pallas as pl
from jax.experimental.pallas import tpu as pltpu
from jax.sharding import PartitionSpec as P

HD = 128
GH = 8
NX, NY, NZ = 4, 8, 8
TOK = 128
D = 8192
HALF = D // 2
BLK = HALF // NZ
SCALE = HD ** (-0.5)
MESH = pl.DeviceIdType.MESH
F32, BF16 = jnp.float32, jnp.bfloat16
NT = (((1,), (1,)), ((), ()))
TN = (((0,), (0,)), ((), ()))
NN = (((1,), (0,)), ((), ()))
K, V = 0, 1
FAR_X = (2, 1, 3, 0)
FAR = (4, 3, 5, 2, 6, 1, 7, 0)


def dot(a, b, dims=NN):
    return lax.dot_general(a, b, dims, preferred_element_type=F32)


def wait_bytes(ref, sem):
    pltpu.make_async_copy(ref, ref, sem).wait()


def kernel(
    tok, q_hbm, go_hbm, seg_hbm, w_hbm, scales_hbm,
    attn, gtok, gw,
    seg, w, scales, X, XT, W, GT, qv, gov, prob_s, low_s, sh, kvs, kvr, G, PB, SB, RB, YS, XR,
    l_sem, tok_sem, ag_d_send, ag_d_recv, ag_send, ag_recv,
    kv_sem, g_sem, gt_sem, rs_send, rs_recv, rs_d_send, rs_d_recv,
):
    node, dev = lax.axis_index("node"), lax.axis_index("dev")
    z, x = node // NX, node % NX
    y, c = dev // 2, dev % 2
    other = 1 - c
    home = x // 2

    def at(x, y, z, c):
        return {"node": z * NX + x, "dev": y * 2 + c}

    def remote(src, dst, ss, rs, target):
        return pltpu.make_async_remote_copy(
            src_ref=src, dst_ref=dst, send_sem=ss, recv_sem=rs, device_id=target, device_id_type=MESH
        )

    def cols(zz, core):
        return pl.ds(pl.multiple_of(zz * 2 * BLK + core * BLK, BLK), BLK)

    mine = pl.ds(pl.multiple_of(c * TOK, TOK), TOK)
    theirs = pl.ds(pl.multiple_of(other * TOK, TOK), TOK)

    small = [
        pltpu.make_async_copy(src, dst, l_sem.at[3 + n])
        for n, (src, dst) in enumerate(((w_hbm, w), (scales_hbm, scales), (seg_hbm, seg)))
    ]
    for copy in small:
        copy.start()

    bar = pltpu.get_barrier_semaphore()

    def greet(device):
        pl.semaphore_signal(bar, inc=1, device_id=device, device_id_type=MESH)

    def gather_target(kx, kk):
        return at((x + kx) % NX, (y + kk * other) % NY, (z + kk * c) % NZ, home)

    def owner(r, xh, kk):
        return at(c * 2 + xh, (y + kk) % NY if r == 0 else y, z if r == 0 else (z + kk) % NZ, r)

    for kk in FAR:
        for kx in FAR_X:
            if kk == 0 and kx == 0:
                @pl.when(home != c)
                def _():
                    greet(gather_target(0, 0))
            else:
                greet(gather_target(kx, kk))
        for r in range(2):
            for xh in range(2):
                if kk == 0:
                    @pl.when(jnp.logical_not((r == c) & (c * 2 + xh == x)))
                    def _():
                        greet(owner(r, xh, 0))
                else:
                    greet(owner(r, xh, kk))
    for step in (1, 2, 6, 7):
        greet(at(x, (y + step) % NY, z, c))
        greet(at(x, y, (z + step) % NZ, c))
    greet(at(x, y, z, other))

    for zz in range(NZ):
        pltpu.make_async_copy(tok.at[:, cols(zz, c)], X.at[zz, mine], l_sem.at[0]).start()
    q_copy = pltpu.make_async_copy(q_hbm, qv, l_sem.at[1])
    go_copy = pltpu.make_async_copy(go_hbm, gov, l_sem.at[2])
    q_copy.start()
    go_copy.start()

    small[0].wait()
    small[1].wait()
    pick = lax.broadcasted_iota(jnp.int32, (1, 4), 1) == z // 2
    scale = jnp.sum(jnp.where(pick, scales[...].astype(F32), 0.0), axis=1, keepdims=True)
    scaled = (w[...].astype(F32) * scale).astype(BF16)
    sh[K] = scaled[:, :HD]
    sh[V] = scaled[:, HD:]

    @pl.when(home == c)
    def _():
        pl.semaphore_wait(bar, 71)

    @pl.when(home != c)
    def _():
        pl.semaphore_wait(bar, 73)

    place = W.at[:, z * 2 + x % 2, y, c]
    for kk in FAR:
        for kx in FAR_X:
            cp = remote(sh, place, ag_d_send, ag_d_recv.at[c], gather_target(kx, kk))
            if kk == 0 and kx == 0:
                @pl.when(home != c)
                def _():
                    cp.start()

                @pl.when(home == c)
                def _():
                    pltpu.make_async_copy(sh, place, ag_d_recv.at[c]).start()
            else:
                cp.start()


    def turn(zz):
        XT[pl.ds(2 * zz, 2)] = X[zz].T.reshape(2, NY, 2, 16, 2 * TOK)

    def piece(p, r, i, sub):
        if r == 0:
            return W.at[p, i * 2 + sub, :, 0]
        return W.at[p, pl.ds(sub * NZ, NZ), i, 1]

    def neighbour(r, step):
        if r == 0:
            return at(x, y, (z + step + NZ) % NZ, c)
        return at(x, (y + step + NY) % NY, z, c)

    pos = (z, y)

    def ag_copy(p, r, d, k, places, sub):
        step = 1 - 2 * d
        part = piece(p, r, (pos[r] - step * k + 8) % 8, sub)
        return remote(part, part, ag_send.at[p], ag_recv.at[p, r, d, k + places - 1, sub], neighbour(r, step * places))

    def ag_arrival(p, r, d, k, sub):
        wait_bytes(piece(p, r, (pos[r] - (1 - 2 * d) * k + 8) % 8, sub), ag_recv.at[p, r, d, k - 1, sub])

    GOES = ({0: (1,), 1: (1,), 2: (2, 1)},) * 2

    def ag_pass(p, k):
        for sub in range(2):
            for r in range(2):
                for d in range(2):
                    if k == 4 and sub != d:
                        continue
                    if k > 0:
                        ag_arrival(p, r, d, k, sub)
                    for places in GOES[p].get(k, ()):
                        if k + places < 4 or sub == d:
                            ag_copy(p, r, d, k, places, sub).start()

    wait_bytes(W.at[:, pl.ds(z * 2, 2), :, 0], ag_d_recv.at[0])
    wait_bytes(W.at[:, :, y, 1], ag_d_recv.at[1])
    ag_pass(K, 0)
    ag_pass(V, 0)

    for zz in range(NZ):
        remote(tok.at[:, cols(zz, other)], X.at[zz, mine], tok_sem.at[0], tok_sem.at[1], at(x, y, z, other)).start()
    ag_pass(K, 1)
    ag_pass(V, 1)
    wait_bytes(X.at[:, mine], l_sem.at[0])
    wait_bytes(X.at[:, theirs], tok_sem.at[1])
    for zz in range(4):
        turn(zz)
    ag_pass(K, 2)
    ag_pass(V, 2)
    for zz in range(4, NZ):
        turn(zz)

    def kv_copy(p):
        return remote(kvs.at[p, theirs], kvr.at[p], kv_sem.at[p], kv_sem.at[2 + p], at(x, y, z, other))

    def rows(p, zz):
        return W[p, pl.ds(2 * zz, 2)].reshape(BLK, HD)

    def project(p):
        ag_pass(p, 3)
        ag_pass(p, 4)
        for part in (theirs, mine):
            acc = jnp.zeros((TOK, HD), F32)
            for zz in range(NZ):
                acc += dot(X[zz, part], rows(p, zz))
            kvs[p, part] = acc
            if part is theirs:
                kv_copy(p).start()

    project(K)
    small[2].wait()
    seg_t = jnp.broadcast_to(seg[...].astype(F32), (TOK, TOK))
    seg_s = seg_t.T
    s_at = lax.broadcasted_iota(jnp.int32, (TOK, TOK), 0)
    t_at = lax.broadcasted_iota(jnp.int32, (TOK, TOK), 1)
    one = jnp.where((s_at <= t_at) & (seg_s == seg_t), 1.0, 0.0)
    allowed = jnp.concatenate([one] * GH, axis=1) > 0.5
    q_copy.wait()
    go_copy.wait()

    def stacked(ref):
        return jnp.concatenate([ref[:, h * HD:(h + 1) * HD] for h in range(GH)], axis=0)

    def g_copy(p):
        return remote(G.at[p, mine], G.at[p, mine], g_sem.at[p], g_sem.at[2 + p], at(x, y, z, other))

    kv_copy(K).wait_recv()
    kb = (kvs[K, mine] + kvr[K]).astype(BF16)
    st = jnp.where(allowed, dot(kb, stacked(qv), NT) * SCALE, -1e30)
    ex = jnp.exp(st - jnp.max(st, axis=0, keepdims=True))
    pr = ex * (1.0 / jnp.sum(ex, axis=0, keepdims=True))
    low = pr.astype(BF16)
    prob_s[...] = pr
    low_s[...] = low
    gv = dot(low, stacked(gov))
    G[V, mine] = gv.astype(BF16)
    g_copy(V).start()

    project(V)

    H = TOK

    def partial(p, r, places):
        i = (pos[r] + places + 8) % 8
        if r == 0:
            lhs = XT[pl.ds(2 * i, 2), :, 0]
        else:
            lhs = XT[:, i, 1]
        return dot(lhs.reshape(2 * TOK, 2 * TOK), G[p])

    def rs_copy(p, r, d, n, sub, places):
        return remote(
            SB.at[p, r, d, n, sub], RB.at[p, r, d, n, sub],
            rs_send.at[p], rs_recv.at[p, r, d, n, sub], neighbour(r, (1 - 2 * d) * places),
        )

    def rs_out(p, r, d, n, sub, places, value):
        SB[p, r, d, n, sub] = value.astype(BF16)
        rs_copy(p, r, d, n, sub, places).start()

    def rs_in(p, r, d, n, sub):
        wait_bytes(RB.at[p, r, d, n, sub], rs_recv.at[p, r, d, n, sub])
        return RB[p, r, d, n, sub].astype(F32)

    def rs_begin(p):
        for r in range(2):
            part = partial(p, r, 4)
            for d in range(2):
                rs_out(p, r, d, 0, d, 2, part[d * H:(d + 1) * H])
        for r in range(2):
            for d in range(2):
                part = partial(p, r, 3 * (1 - 2 * d))
                for sub in range(2):
                    rs_out(p, r, d, 1, sub, 1, part[sub * H:(sub + 1) * H])

    def rs_ahead(p):
        for r in range(2):
            for n, places in enumerate((2, -2, 1, -1, 0)):
                PB[p, r, n] = partial(p, r, places)

    def rs_middle(p):
        for sub in range(2):
            for r in range(2):
                for d in range(2):
                    value = PB[p, r, d, sub * H:(sub + 1) * H] + rs_in(p, r, d, 1, sub)
                    if sub == d:
                        value += rs_in(p, r, d, 0, sub)
                    rs_out(p, r, d, 2, sub, 1, value)

    def rs_near(p):
        for sub in range(2):
            for r in range(2):
                for d in range(2):
                    rs_out(p, r, d, 3, sub, 1, PB[p, r, 2 + d, sub * H:(sub + 1) * H] + rs_in(p, r, d, 2, sub))

    def rs_own(p, r):
        for sub in range(2):
            total = PB[p, r, 4, sub * H:(sub + 1) * H]
            for d in range(2):
                total += rs_in(p, r, d, 3, sub)
            YS[r, pl.ds(sub * 8, 8), p] = total.astype(BF16).reshape(8, 16, HD)

    def rs_direct(r):
        for kk in FAR:
            for xh in range(2):
                if r == 0:
                    src = YS.at[0, xh * 8 + (y + kk) % NY]
                    dst = XR.at[x * 8 + y]
                else:
                    src = YS.at[1, (z + kk) % NZ * 2 + xh]
                    dst = XR.at[x * 8 + z]
                cp = remote(src, dst, rs_d_send, rs_d_recv, owner(r, xh, kk))
                if kk == 0:
                    is_me = (r == c) & (c * 2 + xh == x)

                    @pl.when(jnp.logical_not(is_me))
                    def _():
                        cp.start()

                    @pl.when(is_me)
                    def _():
                        pltpu.make_async_copy(src, dst, rs_d_recv).start()
                else:
                    cp.start()

    wait_bytes(G.at[V, theirs], g_sem.at[2 + V])
    rs_begin(V)

    kv_copy(V).wait_recv()
    vb = (kvs[V, mine] + kvr[V]).astype(BF16)
    pr = prob_s[...]
    dp = dot(vb, stacked(gov), NT)
    inner = jnp.sum(pr * dp, axis=0, keepdims=True)
    gk = dot((pr * (dp - inner) * SCALE).astype(BF16), stacked(qv))
    G[K, mine] = gk.astype(BF16)
    g_copy(K).start()

    def grad_tokens(zz):
        wz = jnp.concatenate([rows(K, zz), rows(V, zz)], axis=1)
        g = jnp.concatenate([G[K], G[V]], axis=1)
        GT[zz] = dot(g, wz, NT).astype(BF16)
        gtok[:, cols(zz, c)] = GT[zz, mine]
        remote(GT.at[zz, theirs], gtok.at[:, cols(zz, c)], gt_sem.at[0], gt_sem.at[1], at(x, y, z, other)).start()

    def attend_out(h):
        attn[:, h * HD:(h + 1) * HD] = dot(low_s[:, h * TOK:(h + 1) * TOK], vb, TN).astype(BF16)

    rs_ahead(V)
    wait_bytes(G.at[K, theirs], g_sem.at[2 + K])
    rs_begin(K)
    rs_middle(V)
    rs_ahead(K)
    rs_middle(K)
    rs_near(V)
    for zz in range(0, 4):
        grad_tokens(zz)
    rs_near(K)
    for zz in range(4, 8):
        grad_tokens(zz)
    for r in range(2):
        rs_own(V, r)
    for r in range(2):
        rs_own(K, r)
        rs_direct(r)
    for h in range(GH):
        attend_out(h)

    for k in range(2):
        wait_bytes(gtok.at[:, pl.ds(0, HALF)], gt_sem.at[k])
    for p in range(2):
        wait_bytes(W.at[p, pl.ds(0, 14)], ag_send.at[p])
        wait_bytes(W.at[p, pl.ds(0, 14)], rs_send.at[p])
        kv_copy(p).wait_send()
        g_copy(p).wait_send()
    wait_bytes(X.at[:, mine], tok_sem.at[0])

    @pl.when(home == c)
    def _():
        wait_bytes(XR.at[pl.ds(0, 31)], ag_d_send)

    @pl.when(home != c)
    def _():
        wait_bytes(XR, ag_d_send)

    wait_bytes(XR, rs_d_recv)
    for p in range(2):
        gw[:, p * HD:(p + 1) * HD] = jnp.sum(XR[:, p].astype(F32), axis=0)

    @pl.when(home == c)
    def _():
        wait_bytes(XR.at[pl.ds(0, 31)], rs_d_send)

    @pl.when(home != c)
    def _():
        wait_bytes(XR, rs_d_send)


OUTS = (((TOK, GH * HD), BF16), ((TOK, D), BF16), ((16, 2 * HD), F32))


def write_out(*refs):
    copies = [pltpu.make_async_copy(refs[i], refs[3 + i], refs[6].at[i]) for i in range(3)]
    for copy in copies:
        copy.start()
    for copy in copies:
        copy.wait()


def shards(tokens, queries, grad_out, seg_ids, w_values, w_scales):
    vmem = pl.BlockSpec(memory_space=pltpu.VMEM)
    hbm = pl.BlockSpec(memory_space=pltpu.HBM)
    dma = pltpu.SemaphoreType.DMA
    inner = pl.pallas_call(
        kernel,
        out_shape=tuple(pltpu.VMEM(shape, dtype) for shape, dtype in OUTS),
        in_specs=[hbm] * 6,
        out_specs=(vmem, vmem, vmem),
        scratch_shapes=[
            pltpu.VMEM((1, TOK), jnp.int32),
            pltpu.VMEM((16, 2 * HD), BF16),
            pltpu.VMEM((1, 4), BF16),
            pltpu.VMEM((NZ, 2 * TOK, BLK), BF16),
            pltpu.VMEM((2 * NZ, NY, 2, 16, 2 * TOK), BF16),
            pltpu.VMEM((2, 2 * NZ, NY, 2, 16, HD), BF16),
            pltpu.VMEM((NZ, 2 * TOK, BLK), BF16),
            pltpu.VMEM((TOK, GH * HD), BF16),
            pltpu.VMEM((TOK, GH * HD), BF16),
            pltpu.VMEM((TOK, GH * TOK), F32),
            pltpu.VMEM((TOK, GH * TOK), BF16),
            pltpu.VMEM((2, 16, HD), BF16),
            pltpu.VMEM((2, 2 * TOK, HD), F32),
            pltpu.VMEM((2, TOK, HD), F32),
            pltpu.VMEM((2, 2 * TOK, HD), BF16),
            pltpu.VMEM((2, 2, 5, 2 * TOK, HD), F32),
            pltpu.VMEM((2, 2, 2, 4, 2, TOK, HD), BF16),
            pltpu.VMEM((2, 2, 2, 4, 2, TOK, HD), BF16),
            pltpu.VMEM((2, 16, 2, 16, HD), BF16),
            pltpu.VMEM((32, 2, 16, HD), BF16),
            dma((6,)), dma((2,)), dma, dma((2,)), dma((2,)), dma((2, 2, 2, 4, 2)),
            dma((4,)), dma((4,)), dma((2,)), dma((2,)), dma((2, 2, 2, 4, 2)), dma, dma,
        ],
        compiler_params=pltpu.CompilerParams(
            collective_id=0, has_side_effects=True, vmem_limit_bytes=60 * 2**20
        ),
        cost_estimate=pl.CostEstimate(flops=2 * 10**9, bytes_accessed=5 * 2**20, transcendentals=131072),
        name="layer",
    )(tokens, queries, grad_out, seg_ids, w_values, w_scales.reshape(1, 4))
    return tuple(pl.pallas_call(
        write_out,
        out_shape=tuple(jax.ShapeDtypeStruct(shape, dtype) for shape, dtype in OUTS),
        in_specs=[vmem] * 3,
        out_specs=(pl.BlockSpec(memory_space=pl.ANY),) * 3,
        scratch_shapes=[dma((3,))],
        compiler_params=pltpu.CompilerParams(vmem_limit_bytes=4 * 2**20),
        name="write_out",
    )(*inner))


def solution(mesh):
    spec = P(("node", "dev"), None)
    return jax.shard_map(
        shards,
        mesh=mesh,
        in_specs=(spec, spec, spec, spec, spec, P()),
        out_specs=(spec, spec, spec),
        check_vma=False,
    )
```
